512 devices in a mesh: dp: 64 (over z_lo, x, y), mp: 8 (over z_hi, core).
Axes of the slice: x: 4, y: 8, z: 8 (z_hi: 4, z_lo: 2; z = z_hi * 2 + z_lo), core: 2. Of those that a mesh axis runs over, the one named last changes fastest.
Arguments:
- hidden: bfloat16 [256, 128, 4096], P('dp', None, 'mp'), may hold values from -6 to 6
- frozen_matrix: bfloat16 [4096, 4096], P('dp', 'mp'), may hold values from -0.09375 to 0.09375
- adapter_down_weight: bfloat16 [4096, 32], P('mp'), may hold values from -0.09375 to 0.09375
- adapter_up_weight: bfloat16 [32, 4096], P(None, 'mp'), may hold values from -1 to 1
- sequence_token_counts: int32 [256], replicated, may hold values from 1 to 128, 20480 in all
- assignment: int32 [256], replicated, may hold values from 0 to 255, each once
- positives: int32 [64], P('dp'), may hold values from 0 to 191
Outputs:
- query_loss: float32 [64], P('dp')
- grad_a: float32 [4096, 32], P('mp')
- grad_b: float32 [32, 4096], P(None, 'mp')
The draws below stay inside these ranges and needn't reach their ends.
All inputs are finite; a program needn't handle non-finite values.
Results may differ from the reference program's by a relative error of at most 0.014.
Values may be sent and summed in bfloat16 or wider, within the bound.
A program may use at most 64 MiB of HBM per device.

```python
import math
import jax
import jax.numpy as jnp
import numpy as np
from jax import lax

MODEL_WIDTH = 4096
ADAPTER_RANK = 32
SEQUENCE_LENGTH = 128
SEQS = 256
NQ = 64
ND = 192


def touch_ends(values, key, least, high):
    index_at = [jax.random.randint(jax.random.fold_in(key, axis), (), 0, length) for axis, length in enumerate(values.shape)]
    longest = values.shape.index(max(values.shape))
    beside = index_at[:longest] + [(index_at[longest] + 1) % values.shape[longest]] + index_at[longest + 1:]
    return values.at[tuple(index_at)].set(least).at[tuple(beside)].set(high)


def level_of(rng, dims, pieces, least, top_value):
    factor_of, own = 1.0, jax.random.fold_in(rng, 6)
    for dim, blocks in pieces:
        draws = jnp.exp(jax.random.uniform(jax.random.fold_in(own, dim), (blocks,), jnp.float32, least / len(pieces), top_value / len(pieces)))
        factor_of = factor_of * jnp.repeat(draws, dims[dim] // blocks).reshape([-1 if axis == dim else 1 for axis in range(len(dims))])
    return factor_of


def length_profile(count, total, most, slope):
    loads = [(1 << 20) // math.isqrt(rank ** slope) + 1 for rank in range(2, count + 1)]
    surplus, given = total - most - (count - 1), [1] * (count - 1)
    while surplus > 0:
        movable = [i for i in range(count - 1) if given[i] < most]
        pool, remaining = sum([loads[i] for i in movable]), surplus
        for i in movable:
            addition = min(most - given[i], max(1, remaining * loads[i] // pool), surplus)
            given[i] = given[i] + addition
            surplus = surplus - addition
    return np.array([most] + given)


def ragged_sizes(stream_key, number_of, total, most, lean):
    if number_of == 2:
        one = jax.random.randint(stream_key, (), max(1, total - most), min(most, total - 1) + 1)
        return jnp.stack([one, total - one])
    sizes = jnp.asarray(length_profile(number_of, total, most, lean), jnp.int32)
    twos = (number_of - 1) // 2
    giver, receiver = sizes[1:1 + 2 * twos:2], sizes[2:2 + 2 * twos:2]
    margin = jnp.minimum(giver - 1, most - receiver)
    shifted = jax.random.randint(jax.random.fold_in(stream_key, 1), (twos,), 0, 1 << 20) % (margin + 1)
    sizes = sizes.at[1:1 + 2 * twos:2].set(giver - shifted).at[2:2 + 2 * twos:2].set(receiver + shifted)
    return sizes[jax.random.permutation(jax.random.fold_in(stream_key, 2), number_of)]


def noise(own_key, dims, deviation, limit, pieces=(), dtype=jnp.bfloat16):
    array = deviation * jax.random.normal(own_key, dims, jnp.float32)
    if pieces:
        array = array * level_of(own_key, dims, pieces, -0.22, 0.18)
    return jnp.clip(array, -limit, limit).astype(dtype)


def setup_inputs(seed: int = 0) -> dict:
    key_list = jax.random.split(jax.random.key(seed), 8)
    return {
        "hidden": noise(key_list[0], (SEQS, SEQUENCE_LENGTH, MODEL_WIDTH), 1.0, 6.0, ((0, 64), (2, 8))),
        "frozen_matrix": noise(key_list[1], (MODEL_WIDTH, MODEL_WIDTH), MODEL_WIDTH ** -0.5, 0.09375, ((0, 64), (1, 8))),
        "adapter_down_weight": noise(key_list[2], (MODEL_WIDTH, ADAPTER_RANK), MODEL_WIDTH ** -0.5, 0.09375, ((0, 8),)),
        "adapter_up_weight": noise(key_list[3], (ADAPTER_RANK, MODEL_WIDTH), ADAPTER_RANK ** -0.5, 1.0, ((1, 8),)),
        "sequence_token_counts": ragged_sizes(key_list[4], SEQS, SEQS * SEQUENCE_LENGTH * 5 // 8, SEQUENCE_LENGTH, 2).astype(jnp.int32),
        "assignment": jax.random.permutation(key_list[5], SEQS).astype(jnp.int32),
        "positives": touch_ends(jax.random.randint(key_list[6], (NQ,), 0, ND), jax.random.fold_in(key_list[6], 1), 0, ND - 1).astype(jnp.int32),
    }


score_scale = 20.0
adapter_factor_scale = 2.0

def encode_layer_block(slot_token_block, frozen_matrix, adapter_down_weight, adapter_up_weight):
    flattened_tokens = slot_token_block.reshape(-1, MODEL_WIDTH)
    rank_projection = jnp.dot(flattened_tokens, adapter_down_weight, preferred_element_type=jnp.float32).astype(jnp.bfloat16)
    hidden_before_norm = flattened_tokens.astype(jnp.float32) + jnp.dot(flattened_tokens, frozen_matrix, preferred_element_type=jnp.float32)
    hidden_before_norm = hidden_before_norm + adapter_factor_scale * jnp.dot(rank_projection, adapter_up_weight, preferred_element_type=jnp.float32)
    inverse_root_square = lax.rsqrt(lax.optimization_barrier(jnp.sum(hidden_before_norm * hidden_before_norm, axis=1, keepdims=True)) / MODEL_WIDTH + 1e-05)
    return (flattened_tokens, rank_projection, hidden_before_norm * inverse_root_square, inverse_root_square)

def reference(hidden, frozen_matrix, adapter_down_weight, adapter_up_weight, sequence_token_counts, assignment, positives):
    slot_lengths = sequence_token_counts[assignment]
    positions = jnp.arange(SEQUENCE_LENGTH).astype(jnp.int32)
    valid_mask = jnp.where(positions[None, :] < slot_lengths[:, None], 1.0, 0.0).astype(jnp.float32)
    pooling_weight = valid_mask / slot_lengths[:, None].astype(jnp.float32)
    hidden_groups = hidden.reshape(SEQS // 8, 8, SEQUENCE_LENGTH, MODEL_WIDTH)
    weight_groups = pooling_weight.reshape(SEQS // 8, 8, SEQUENCE_LENGTH)

    def pool_group(pair):
        slot_token_block, slot_pooling_weight = pair
        flattened_tokens, rank_projection, normalized_rows, inverse_root_square = encode_layer_block(slot_token_block, frozen_matrix, adapter_down_weight, adapter_up_weight)
        return jnp.einsum('xw,xwm->xm', slot_pooling_weight, normalized_rows.reshape(8, SEQUENCE_LENGTH, MODEL_WIDTH))
    pooled_embedding = lax.map(pool_group, (hidden_groups, weight_groups)).reshape(SEQS, MODEL_WIDTH)
    pooled_norm = jnp.sqrt(lax.optimization_barrier(jnp.sum(pooled_embedding * pooled_embedding, axis=1, keepdims=True)) + 1e-06)
    unit = pooled_embedding / pooled_norm
    inverse = jnp.argsort(assignment).astype(jnp.int32)
    by_number = unit[inverse]
    queries = by_number[:NQ]
    documents = by_number[NQ:]
    scores = score_scale * jnp.dot(queries, documents.T, precision=lax.Precision.HIGHEST, preferred_element_type=jnp.float32)
    exponents = jnp.exp(scores)
    exp_total = lax.optimization_barrier(jnp.sum(exponents, axis=1))
    positive_mask = (jnp.arange(ND).astype(jnp.int32)[None, :] == positives[:, None]).astype(jnp.float32)
    positive_score = lax.optimization_barrier(jnp.sum(positive_mask * scores, axis=1))
    query_loss = jnp.log(exp_total) - positive_score
    score_grads = exponents / exp_total[:, None] - positive_mask
    grad_queries = score_scale * jnp.dot(score_grads, documents, precision=lax.Precision.HIGHEST, preferred_element_type=jnp.float32)
    grad_documents = score_scale * jnp.dot(score_grads.T, queries, precision=lax.Precision.HIGHEST, preferred_element_type=jnp.float32)
    grad_by_number = jnp.concatenate([grad_queries, grad_documents], axis=0)
    grad_unit = grad_by_number[assignment]
    inner = lax.optimization_barrier(jnp.sum(unit * grad_unit, axis=1, keepdims=True))
    grad_pooled = (grad_unit - unit * inner) / pooled_norm

    def backward_group(carry, triple):
        slot_token_block, slot_pooling_weight, slot_grads = triple
        flattened_tokens, rank_projection, normalized_rows, inverse_root_square = encode_layer_block(slot_token_block, frozen_matrix, adapter_down_weight, adapter_up_weight)
        grad_normed = (slot_pooling_weight[:, :, None] * slot_grads[:, None, :]).reshape(-1, MODEL_WIDTH)
        dot_mean = lax.optimization_barrier(jnp.sum(grad_normed * normalized_rows, axis=1, keepdims=True)) / MODEL_WIDTH
        prenorm_gradient = (inverse_root_square * (grad_normed - normalized_rows * dot_mean)).astype(jnp.bfloat16)
        low_rank_gradient = (adapter_factor_scale * jnp.dot(prenorm_gradient, adapter_up_weight.T, preferred_element_type=jnp.float32)).astype(jnp.bfloat16)
        part_a = jnp.dot(flattened_tokens.T, low_rank_gradient, preferred_element_type=jnp.float32)
        part_b = adapter_factor_scale * jnp.dot(rank_projection.T, prenorm_gradient, preferred_element_type=jnp.float32)
        return ((carry[0] + part_a, carry[1] + part_b), None)
    start_grads = (jnp.zeros((MODEL_WIDTH, ADAPTER_RANK), jnp.float32), jnp.zeros((ADAPTER_RANK, MODEL_WIDTH), jnp.float32))
    (grad_a, grad_b), unused = lax.scan(backward_group, start_grads, (hidden_groups, weight_groups, grad_pooled.reshape(SEQS // 8, 8, MODEL_WIDTH)))
    return (query_loss, grad_a, grad_b)
```

```python
import jax
import jax.numpy as jnp
from jax import lax
from jax.experimental import pallas as pl
from jax.experimental.pallas import tpu as pltpu
from jax.sharding import PartitionSpec as P

MESH = pl.DeviceIdType.MESH
F32, BF16 = jnp.float32, jnp.bfloat16
score_scale = 20.0
adapter_factor_scale = 2.0
WIDTH = 4096
TAGS = 176

NN = (((1,), (0,)), ((), ()))
NT = (((1,), (1,)), ((), ()))


def mm(left, right, dims=NN):
    return lax.dot_general(left, right, dims, preferred_element_type=F32)


def mm_exact(left, right, dims=NN):
    return lax.dot_general(left, right, dims, precision=lax.Precision.HIGHEST, preferred_element_type=F32)


def split_rows(value):
    high = value.astype(BF16).astype(F32)
    return jnp.concatenate([high, value - high], axis=0).astype(BF16)


def mm_split(value, right, dims=NN):
    rows = value.shape[0]
    both = mm(split_rows(value), right, dims)
    return both[:rows] + both[rows:]


def kernel(
    h, w, a, b, pos, counts, assign, assign_row,
    loss, grad_a, grad_b,
    hid, wf, low_part, low_recv, low_full, pb,
    acc, pre, sq_row, one_hot, sq, p_part, p_recv, p_full,
    pooled, units, x_part, x_recv, x_full, n_recv, ex,
    f_part, f_recv, f_mid, f_out,
    send_sem, recv_sem,
):
    dp, mp = lax.axis_index("dp"), lax.axis_index("mp")
    y = lax.rem(dp, 8)
    zx = lax.div(dp, 8)
    zl, x = lax.div(zx, 4), lax.rem(zx, 4)
    zh, core = lax.div(mp, 2), lax.rem(mp, 2)
    sib = zh * 2 + 1 - core
    up, down = lax.rem(zh + 1, 4) * 2 + core, lax.rem(zh + 3, 4) * 2 + core
    far = lax.rem(zh + 2, 4) * 2 + core
    sib_up, sib_down = lax.rem(zh + 1, 4) * 2 + 1 - core, lax.rem(zh + 3, 4) * 2 + 1 - core
    sib_far = lax.rem(zh + 2, 4) * 2 + 1 - core

    index_of = {"mp": mp, "y": y, "zx": zx}
    device_of = {
        "mp": lambda p: (dp, p),
        "y": lambda p: (zx * 8 + p, mp),
        "zx": lambda p: (p * 8 + y, mp),
    }
    used = [0]
    started = []

    def tag():
        used[0] += 1
        return used[0] - 1

    def remote(src, dst, number, device):
        return pltpu.make_async_remote_copy(
            src_ref=src, dst_ref=dst, send_sem=send_sem.at[number], recv_sem=recv_sem.at[number],
            device_id=device, device_id_type=MESH,
        )

    def send(src, dst, number, device):
        copy = remote(src, dst, number, device)
        copy.start()
        started.append(copy)

    def landed(region, number):
        remote(region, region, number, (dp, sib)).wait_recv()

    def spread(kind, src, dst):
        me, numbers = index_of[kind], []
        for k in range(1, 8):
            peer = lax.rem(me + k, 8)
            numbers.append(tag())
            send(src(peer), dst, numbers[-1], device_of[kind](peer))
        return numbers

    def collect(kind, numbers, region):
        for k in range(1, 8):
            landed(region(lax.rem(index_of[kind] + 8 - k, 8)), numbers[k - 1])

    barrier = pltpu.get_barrier_semaphore()
    for kind in ("mp", "y", "zx"):
        for k in range(1, 8):
            pl.semaphore_signal(barrier, inc=1, device_id=device_of[kind](lax.rem(index_of[kind] + k, 8)), device_id_type=MESH)
    wf[zl, x, y] = w[...]
    pb[zx, y] = jnp.full((1, 128), pos[0].astype(F32), F32)
    pl.semaphore_wait(barrier, 21)

    w_z = tag()
    send(w, wf.at[zl, x, y], w_z, ((1 - zl) * 32 + x * 8 + y, mp))

    def part(q, n=1):
        return pl.ds(128 * q, 128 * n)

    h_up, h_down = [tag() for _ in range(4)], [tag() for _ in range(4)]
    h_sib = tag()
    for q in range(4):
        send(h.at[part(q)], hid.at[mp, part(q)], h_up[q], (dp, up))
        send(h.at[part(3 - q)], hid.at[mp, part(3 - q)], h_down[3 - q], (dp, down))
    send(h, hid.at[mp], h_sib, (dp, sib))

    low_t = mm(h[...], a[...]).T
    for o in range(8):
        low_part[o] = low_t[16 * (o // 4) : 16 * (o // 4) + 16, 128 * (o % 4) : 128 * (o % 4) + 128]
    low_tags = spread("mp", lambda p: low_part.at[p], low_recv.at[mp])
    low_recv[mp] = low_part[mp]
    pos_y = spread("y", lambda p: pb.at[zx, y], pb.at[zx, y])

    row_of = lax.broadcasted_iota(jnp.int32, (256, 1024), 0)
    col_of = lax.broadcasted_iota(jnp.int32, (256, 1024), 1)
    slot_of = (lax.div(col_of, 16) * 4 + lax.rem(col_of, 4) == row_of).astype(BF16)
    numbers8 = jnp.broadcast_to(assign_row[...].astype(F32), (8, 256)).astype(BF16)
    number_of = mm(numbers8, slot_of)[0:1].astype(jnp.int32)
    quarter = lax.rem(lax.div(col_of, 4), 4)
    for j in range(4):
        one_hot[j] = jnp.where(quarter == j, (row_of == number_of).astype(F32), 0.0).astype(BF16)

    def ring_x(view):
        tags = [tag() for _ in range(6)]

        def first():
            send(view(x, 0), view(x, 0), tags[0], (device_x(1)))
            send(view(x, 1), view(x, 1), tags[1], (device_x(3)))
            send(view(x, 1), view(x, 1), tags[2], (device_x(1)))
            send(view(x, 0), view(x, 0), tags[3], (device_x(3)))

        def second():
            landed(view(lax.rem(x + 3, 4), 0), tags[0])
            send(view(lax.rem(x + 3, 4), 0), view(lax.rem(x + 3, 4), 0), tags[4], device_x(1))
            landed(view(lax.rem(x + 1, 4), 1), tags[1])
            send(view(lax.rem(x + 1, 4), 1), view(lax.rem(x + 1, 4), 1), tags[5], device_x(3))

        def last():
            landed(view(lax.rem(x + 3, 4), 1), tags[2])
            landed(view(lax.rem(x + 1, 4), 0), tags[3])
            landed(view(lax.rem(x + 2, 4), 0), tags[4])
            landed(view(lax.rem(x + 2, 4), 1), tags[5])

        return first, second, last

    def device_x(k):
        return (zl * 32 + lax.rem(x + k, 4) * 8 + y, mp)

    def device_y(k):
        return (zx * 8 + lax.rem(y + k, 8), mp)

    def ring_y(whole, half):
        ups, downs = [tag() for _ in range(4)], [tag() for _ in range(4)]

        def step(j):
            below, above = lax.rem(y + 8 - j, 8), lax.rem(y + j, 8)
            if 0 < j < 4:
                landed(whole(below), ups[j - 1])
                landed(whole(above), downs[j - 1])
            if j < 3:
                send(whole(below), whole(below), ups[j], device_y(1))
                send(whole(above), whole(above), downs[j], device_y(7))
            elif j == 3:
                send(half(below, 0), half(below, 0), ups[3], device_y(1))
                send(half(above, 1), half(above, 1), downs[3], device_y(7))
            else:
                landed(half(below, 0), ups[3])
                landed(half(above, 1), downs[3])

        return step

    rows_a, rows_b = pl.ds(0, 32), pl.ds(32, 32)
    a_x = ring_x(lambda xx, z: wf.at[z, xx, y, rows_a])
    a_y = ring_y(lambda yy: wf.at[:, :, yy, rows_a], lambda yy, z: wf.at[z, :, yy, rows_a])
    b_y = ring_y(lambda yy: wf.at[:, x, yy, rows_b], lambda yy, z: wf.at[z, x, yy, rows_b])
    b_x = ring_x(lambda xx, z: wf.at[z, xx, :, rows_b])

    f_up, f_down = [tag() for _ in range(2)], [tag() for _ in range(2)]
    s_tags = {key: tag() for key in ("d0", "d1", "u0", "u1", "f0", "f1")}

    def pass_on(q):
        landed(hid.at[down, part(q)], h_up[q])
        send(hid.at[down, part(q)], hid.at[down, part(q)], f_up[q], (dp, up))
        landed(hid.at[up, part(3 - q)], h_down[3 - q])
        send(hid.at[up, part(3 - q)], hid.at[up, part(3 - q)], f_down[q], (dp, down))

    def to_sib(owner, half, key):
        send(hid.at[owner, part(2 * half, 2)], hid.at[owner, part(2 * half, 2)], s_tags[key], (dp, sib))

    landed(wf.at[1 - zl, x, y], w_z)
    a_x[0]()
    b_y(0)
    b_y(1)
    a_x[1]()
    a_x[2]()
    a_y(0)
    b_y(2)
    collect("y", pos_y, lambda s: pb.at[zx, s])
    pos_zx = spread("zx", lambda p: pb.at[zx], pb.at[zx])
    b_y(3)
    pass_on(0)
    collect("mp", low_tags, lambda s: low_recv.at[s])
    low_full[mp] = jnp.sum(low_recv[...], axis=0).astype(BF16)
    low_all = spread("mp", lambda p: low_full.at[mp], low_full.at[mp])
    b_y(4)
    b_x[0]()
    pass_on(1)
    to_sib(down, 0, "d0")
    to_sib(up, 1, "u1")
    a_y(1)
    b_x[1]()
    a_y(2)
    for q in (2, 3):
        landed(hid.at[down, part(q)], h_up[q])
        landed(hid.at[up, part(3 - q)], h_down[3 - q])
    to_sib(down, 1, "d1")
    to_sib(up, 0, "u0")
    a_y(3)
    collect("mp", low_all, lambda s: low_full.at[s])
    collect("zx", pos_zx, lambda s: pb.at[s])
    landed(hid.at[sib], h_sib)
    b_x[2]()
    a_y(4)

    def slab(m):
        return wf[lax.div(m, 4), lax.rem(m, 4)].reshape(512, 512)

    def tokens(i):
        return pl.ds(pl.multiple_of(256 * i, 256), 256)

    @pl.loop(0, 2)
    def _(i):
        t = tokens(i)
        acc[t] = mm(h[t], slab(mp)) + mm(hid[sib, t], slab(sib))

    for q in range(2):
        landed(hid.at[far, part(q)], f_up[q])
    to_sib(far, 0, "f0")
    for q in range(2):
        landed(hid.at[far, part(3 - q)], f_down[q])
    to_sib(far, 1, "f1")
    landed(hid.at[sib_down, part(0, 2)], s_tags["d0"])
    landed(hid.at[sib_up, part(2, 2)], s_tags["u1"])
    landed(hid.at[sib_down, part(2, 2)], s_tags["d1"])
    landed(hid.at[sib_up, part(0, 2)], s_tags["u0"])

    @pl.loop(0, 2)
    def _(i):
        t = tokens(i)
        total = acc[t]
        for m in (down, up, sib_down, sib_up):
            total += mm(hid[m, t], slab(m))
        acc[t] = total

    landed(hid.at[sib_far, part(0, 2)], s_tags["f0"])
    landed(hid.at[sib_far, part(2, 2)], s_tags["f1"])

    def joined(ref):
        halves = [jnp.concatenate([ref[4 * r + t] for t in range(4)], axis=1) for r in range(2)]
        return jnp.concatenate(halves, axis=0)

    low = joined(low_full)
    low_rows = low.astype(F32).T.astype(BF16)
    acc[...] += adapter_factor_scale * mm(low_rows, b[...])
    ones = jnp.ones((8, 128), BF16)

    @pl.loop(0, 2)
    def _(i):
        t = tokens(i)
        total = acc[t] + h[t].astype(F32)
        for m in (far, sib_far):
            total += mm(hid[m, t], slab(m))
        pre[t] = total.astype(BF16)
        squares = total * total
        squares = squares[:, 0:128] + squares[:, 128:256] + squares[:, 256:384] + squares[:, 384:512]
        high = squares.astype(BF16)
        rest = (squares - high.astype(F32)).astype(BF16)
        sq_row[i] = mm(ones, high, NT) + mm(ones, rest, NT)

    row8 = lax.broadcasted_iota(jnp.int32, (8, 128), 0)
    lane8 = lax.broadcasted_iota(jnp.int32, (8, 128), 1)

    def by_sequence(wide):
        value = jnp.zeros((8, 128), F32)
        for s in range(4):
            value = jnp.where(lax.rem(row8, 4) == s, wide[:, 128 * s : 128 * s + 128], value)
        return value

    def diagonal(value, first, every):
        keep = lax.rem(row8, 4) if every else row8 - first
        return jnp.concatenate([jnp.where(keep == s, value, 0.0) for s in range(4)], axis=1)

    sq[mp] = by_sequence(jnp.concatenate([sq_row[0], sq_row[1]], axis=1))
    sq_tags = spread("mp", lambda p: sq.at[mp], sq.at[mp])

    p_t = mm(b[...], pre[...], NT)
    for o in range(8):
        p_part[o] = p_t[16 * (o // 4) : 16 * (o // 4) + 16, 128 * (o % 4) : 128 * (o % 4) + 128]
    p_tags = spread("mp", lambda p: p_part.at[p], p_recv.at[mp])
    p_recv[mp] = p_part[mp]

    lengths = jnp.zeros((8, 128), jnp.int32)
    mine = jnp.zeros((8, 256), jnp.int32)
    row256 = lax.broadcasted_iota(jnp.int32, (8, 256), 0)
    lane256 = lax.broadcasted_iota(jnp.int32, (8, 256), 1)
    for s in range(4):
        number = assign[dp * 4 + s]
        lengths = jnp.where(lax.rem(row8, 4) == s, counts[number], lengths)
        mine = jnp.where(lax.rem(row256, 4) == s, number, mine)
    weight = jnp.where(lane8 < lengths, 1.0, 0.0) / lengths.astype(F32)

    collect("mp", sq_tags, lambda s: sq.at[s])
    inv_rms = lax.rsqrt(jnp.sum(sq[...], axis=0) / WIDTH + 1e-05)
    alpha = weight * inv_rms
    mean = mm_split(diagonal(alpha, 0, True), pre[...])
    tile = [
        jnp.where(row8 < 4, mean[:, 256 * j : 256 * j + 128], mean[:, 256 * j + 128 : 256 * j + 256])
        for j in range(2)
    ]
    pooled[zx, y] = jnp.concatenate(tile, axis=0).astype(BF16)

    y_tags = spread("y", lambda p: pooled.at[zx, y], pooled.at[zx, y])
    collect("mp", p_tags, lambda s: p_recv.at[s])
    p_full[mp] = jnp.sum(p_recv[...], axis=0).astype(BF16)
    p_all = spread("mp", lambda p: p_full.at[mp], p_full.at[mp])
    collect("y", y_tags, lambda s: pooled.at[zx, s])
    zx_tags = spread("zx", lambda p: pooled.at[zx], pooled.at[zx])
    collect("zx", zx_tags, lambda s: pooled.at[s])
    gathered = pooled[...].reshape(1024, 128)
    for j in range(4):
        units[:, 128 * j : 128 * j + 128] = mm(one_hot[j], gathered).astype(BF16)

    x_part[...] = mm(units[0:64], units[...], NT).reshape(8, 8, 256)
    x_tags = spread("mp", lambda p: x_part.at[p], x_recv.at[mp])
    square = units[...].astype(F32)
    square = square * square
    high = square.astype(BF16)
    rest = (square - high.astype(F32)).astype(BF16)
    ones_wide = jnp.ones((8, 512), BF16)
    n_recv[mp] = (mm(ones_wide, high, NT) + mm(ones_wide, rest, NT))[0:1]
    n_tags = spread("mp", lambda p: n_recv.at[mp], n_recv.at[mp])
    x_recv[mp] = x_part[mp]
    collect("mp", x_tags, lambda s: x_recv.at[s])
    x_full[mp] = jnp.sum(x_recv[...], axis=0)
    g_tags = spread("mp", lambda p: x_full.at[mp], x_full.at[mp])
    collect("mp", n_tags, lambda s: n_recv.at[s])
    lengths_sq = n_recv[0]
    for s in range(1, 8):
        lengths_sq = lengths_sq + n_recv[s]
    inv_norm = 1.0 / jnp.sqrt(lengths_sq + 1e-06)
    rowq = lax.broadcasted_iota(jnp.int32, (64, 256), 0)
    laneq = lax.broadcasted_iota(jnp.int32, (64, 256), 1)
    inv_query = jnp.sum(jnp.where(rowq == laneq, inv_norm, 0.0), axis=1, keepdims=True)
    scale = score_scale * inv_query * inv_norm
    document = laneq >= 64
    positive = pb[...].reshape(64, 1, 128)[:, 0, :]
    positive = jnp.concatenate([positive, positive], axis=1)
    positive_mask = jnp.where((laneq - 64).astype(F32) == positive, 1.0, 0.0)
    collect("mp", g_tags, lambda s: x_full.at[s])

    scores = jnp.where(document, scale * x_full[...].reshape(64, 256), 0.0)
    exponents = jnp.where(document, jnp.exp(scores), 0.0)
    exp_total = jnp.sum(exponents, axis=1, keepdims=True)
    query_loss = jnp.log(exp_total) - jnp.sum(positive_mask * scores, axis=1, keepdims=True)
    loss[0] = jnp.sum(jnp.where(rowq[:, 0:1] == dp, query_loss, 0.0))
    score_grads = exponents / exp_total - positive_mask
    inner = score_grads * scores
    inner_query = jnp.sum(inner, axis=1, keepdims=True)
    inner_document = jnp.sum(inner, axis=0, keepdims=True)
    coef = scale * score_grads

    below = jnp.zeros((192, 256), F32)
    coef_query = coef - jnp.where(rowq == laneq, inner_query * inv_query * inv_query, 0.0)
    own = (lane256 == mine).astype(F32)
    own_document = jnp.where(lane256 >= 64, own, 0.0)

    def picked(rows, matrix, dims):
        matrix = jnp.concatenate([matrix, below], axis=0)
        top = matrix.astype(BF16)
        return mm(rows, top, dims) + mm(rows, (matrix - top.astype(F32)).astype(BF16), dims)

    mix = (
        picked(own.astype(BF16), coef_query, NN)
        + picked(own_document.astype(BF16), coef, NT)
        - own_document * (inner_document * inv_norm * inv_norm)
    )
    grad = mm_split(mix, units[...])

    b_wide = jnp.concatenate([b[...].astype(F32), jnp.zeros((96, 512), F32)], axis=0).astype(BF16)
    ex[mp] = jnp.where(row8 < 4, by_sequence(mm_split(grad, pre[...], NT)), mm_split(grad, b_wide, NT))
    e_tags = spread("mp", lambda p: ex.at[mp], ex.at[mp])
    alpha_top, alpha_low = diagonal(alpha, 0, False), diagonal(alpha, 4, False)
    low_grad = mm_exact(mm_exact(low.astype(F32), alpha_top, NT), grad)
    collect("mp", p_all, lambda s: p_full.at[s])
    p_rows = joined(p_full).astype(F32)
    collect("mp", e_tags, lambda s: ex.at[s])
    total = jnp.sum(ex[...], axis=0)
    beta = inv_rms * inv_rms * alpha * total / WIDTH
    beta_row = jnp.sum(diagonal(beta, 0, False), axis=0, keepdims=True)
    up_grad = mm_exact(total.T[0:32], alpha_low)
    grad_low = (adapter_factor_scale * (up_grad - p_rows * beta_row)).astype(BF16)
    part_a = mm(grad_low, h[...])
    part_b = adapter_factor_scale * (low_grad - mm((low.astype(F32) * beta_row).astype(BF16), pre[...]))

    f_part[0:4] = part_a.reshape(4, 8, 512)
    f_part[4:8] = part_b.reshape(4, 8, 512)
    tags1 = spread("y", lambda p: f_part.at[p], f_recv.at[y])
    f_recv[y] = f_part[y]
    collect("y", tags1, lambda s: f_recv.at[s])
    f_mid[zx] = jnp.sum(f_recv[...], axis=0)
    tags2 = spread("zx", lambda p: f_mid.at[zx], f_mid.at[zx])
    collect("zx", tags2, lambda s: f_mid.at[s])
    f_out[y] = jnp.sum(f_mid[...], axis=0)
    tags3 = spread("y", lambda p: f_out.at[y], f_out.at[y])
    collect("y", tags3, lambda s: f_out.at[s])
    grad_a[...] = f_out[0:4].reshape(32, 512).T
    grad_b[...] = f_out[4:8].reshape(32, 512)

    for copy in started:
        copy.wait_send()


def body(hidden, frozen_matrix, adapter_down_weight, adapter_up_weight, sequence_token_counts, assignment, positives):
    vmem, smem = pl.BlockSpec(memory_space=pltpu.VMEM), pl.BlockSpec(memory_space=pltpu.SMEM)
    V = pltpu.VMEM
    return pl.pallas_call(
        kernel,
        out_shape=(
            jax.ShapeDtypeStruct((1,), F32),
            jax.ShapeDtypeStruct((512, 32), F32),
            jax.ShapeDtypeStruct((32, 512), F32),
        ),
        in_specs=[vmem, vmem, vmem, vmem, smem, smem, smem, vmem],
        out_specs=(smem, vmem, vmem),
        scratch_shapes=[
            V((8, 512, 512), BF16),
            V((2, 4, 8, 64, 512), BF16),
            V((8, 16, 128), F32),
            V((8, 16, 128), F32),
            V((8, 16, 128), BF16),
            V((8, 8, 1, 128), F32),
            V((512, 512), F32),
            V((512, 512), BF16),
            V((2, 8, 256), F32),
            V((4, 256, 1024), BF16),
            V((8, 8, 128), F32),
            V((8, 16, 128), F32),
            V((8, 16, 128), F32),
            V((8, 16, 128), BF16),
            V((8, 8, 16, 128), BF16),
            V((256, 512), BF16),
            V((8, 8, 256), F32),
            V((8, 8, 256), F32),
            V((8, 8, 256), F32),
            V((8, 1, 256), F32),
            V((8, 8, 128), F32),
            V((8, 8, 512), F32),
            V((8, 8, 512), F32),
            V((8, 8, 512), F32),
            V((8, 8, 512), F32),
            pltpu.SemaphoreType.DMA((TAGS,)),
            pltpu.SemaphoreType.DMA((TAGS,)),
        ],
        compiler_params=pltpu.CompilerParams(
            collective_id=0, has_side_effects=True, vmem_limit_bytes=48 * 1024 * 1024
        ),
    )(
        hidden.reshape(512, 512),
        frozen_matrix,
        adapter_down_weight,
        adapter_up_weight,
        positives,
        sequence_token_counts,
        assignment,
        assignment.reshape(1, 256),
    )


def solution(mesh):
    return jax.shard_map(
        body,
        mesh=mesh,
        in_specs=(
            P("dp", None, "mp"),
            P("dp", "mp"),
            P("mp", None),
            P(None, "mp"),
            P(),
            P(),
            P("dp"),
        ),
        out_specs=(P("dp"), P("mp", None), P(None, "mp")),
        check_vma=False,
    )
```

```python
import jax
import jax.numpy as jnp
from jax import lax
from jax.experimental import pallas as pl
from jax.experimental.pallas import tpu as pltpu
from jax.sharding import PartitionSpec as P

MESH = pl.DeviceIdType.MESH
F32, BF16 = jnp.float32, jnp.bfloat16
score_scale = 20.0
adapter_factor_scale = 2.0
WIDTH = 4096
TAGS = 74

NN = (((1,), (0,)), ((), ()))
NT = (((1,), (1,)), ((), ()))


def mm(left, right, dims=NN):
    return lax.dot_general(left, right, dims, preferred_element_type=F32)


def mm_exact(left, right, dims=NN):
    return lax.dot_general(left, right, dims, precision=lax.Precision.HIGHEST, preferred_element_type=F32)


def split_rows(value):
    high = value.astype(BF16).astype(F32)
    return jnp.concatenate([high, value - high], axis=0).astype(BF16)


def mm_split(value, right, dims=NN):
    rows = value.shape[0]
    both = mm(split_rows(value), right, dims)
    return both[:rows] + both[rows:]


def kernel(
    h_in, w_in, a_in, b_in, pos, counts, assign, assign_row,
    loss, grad_a, grad_b,
    h, w, a, b, hid, wf, low_part, low_recv, low_full, pb,
    acc, pre, sq_row, one_hot, sq, p_part, p_recv, p_full,
    pooled, units, x_part, x_recv, x_full, n_recv, ex,
    f_part, f_recv, f_mid, f_out,
    send_sem, recv_sem, load_sem,
):
    dp, mp = lax.axis_index("dp"), lax.axis_index("mp")
    y = lax.rem(dp, 8)
    zx = lax.div(dp, 8)
    zl, x = lax.div(zx, 4), lax.rem(zx, 4)
    zh, core = lax.div(mp, 2), lax.rem(mp, 2)
    sib = zh * 2 + 1 - core
    up, down = lax.rem(zh + 1, 4) * 2 + core, lax.rem(zh + 3, 4) * 2 + core
    far = lax.rem(zh + 2, 4) * 2 + core
    sib_up, sib_down = lax.rem(zh + 1, 4) * 2 + 1 - core, lax.rem(zh + 3, 4) * 2 + 1 - core
    sib_far = lax.rem(zh + 2, 4) * 2 + 1 - core

    index_of = {"mp": mp, "y": y, "zx": zx}
    device_of = {
        "mp": lambda p: (dp, p),
        "y": lambda p: (zx * 8 + p, mp),
        "zx": lambda p: (p * 8 + y, mp),
    }
    used = [0]
    started = []

    def tag():
        used[0] += 1
        return used[0] - 1

    def remote(src, dst, number, device):
        return pltpu.make_async_remote_copy(
            src_ref=src, dst_ref=dst, send_sem=send_sem.at[number], recv_sem=recv_sem.at[number],
            device_id=device, device_id_type=MESH,
        )

    def send(src, dst, number, device):
        copy = remote(src, dst, number, device)
        copy.start()
        started.append(copy)

    def landed(region, number):
        remote(region, region, number, (dp, sib)).wait_recv()

    def spread(kind, src, dst, seven):
        me, number = index_of[kind], tag()
        for k in range(1, 8):
            peer = lax.rem(me + k, 8)
            remote(src(peer), dst, number, device_of[kind](peer)).start()
        started.append(remote(seven, seven, number, (dp, sib)))
        return number, seven

    def collect(ticket):
        landed(ticket[1], ticket[0])

    loads = [
        pltpu.make_async_copy(src, dst, load_sem.at[i])
        for i, (src, dst) in enumerate(((w_in, w), (h_in, h), (a_in, a), (b_in, b)))
    ]

    barrier = pltpu.get_barrier_semaphore()
    for kind in ("mp", "y", "zx"):
        for k in range(1, 8):
            pl.semaphore_signal(barrier, inc=1, device_id=device_of[kind](lax.rem(index_of[kind] + k, 8)), device_id_type=MESH)
    for copy in loads:
        copy.start()
    pb[zx, y] = jnp.full((1, 128), pos[0].astype(F32), F32)
    first7 = pl.ds(0, 7)
    loads[0].wait()
    wf[zl, x, y] = w[...]
    for copy in loads[1:]:
        copy.wait()
    low_t = mm(a[...], h[...], NT)
    for o in range(8):
        low_part[o] = low_t[16 * (o // 4) : 16 * (o // 4) + 16, 128 * (o % 4) : 128 * (o % 4) + 128].astype(BF16)
    low_recv[mp] = low_part[mp]
    pl.semaphore_wait(barrier, 21)

    w_z = tag()
    send(w, wf.at[zl, x, y], w_z, ((1 - zl) * 32 + x * 8 + y, mp))

    low_tags = spread("mp", lambda p: low_part.at[p], low_recv.at[mp], low_recv.at[first7])

    def half(q):
        return pl.ds(256 * q, 256)

    pos_y = spread("y", lambda p: pb.at[zx, y], pb.at[zx, y], pb.at[zx, first7])

    def device_x(k):
        return (zl * 32 + lax.rem(x + k, 4) * 8 + y, mp)

    def device_y(k):
        return (zx * 8 + lax.rem(y + k, 8), mp)

    def ring_x(view):
        tags = [tag() for _ in range(6)]
        before, after, across = lax.rem(x + 3, 4), lax.rem(x + 1, 4), lax.rem(x + 2, 4)

        def first():
            send(view(x, 0), view(x, 0), tags[0], device_x(1))
            send(view(x, 1), view(x, 1), tags[1], device_x(3))
            send(view(x, 1), view(x, 1), tags[2], device_x(1))
            send(view(x, 0), view(x, 0), tags[3], device_x(3))

        def second():
            landed(view(before, 0), tags[0])
            send(view(before, 0), view(before, 0), tags[4], device_x(1))
            landed(view(after, 1), tags[1])
            send(view(after, 1), view(after, 1), tags[5], device_x(3))

        def last():
            landed(view(before, 1), tags[2])
            landed(view(after, 0), tags[3])
            landed(view(across, 0), tags[4])
            landed(view(across, 1), tags[5])

        return first, second, last

    def ring_y(chunk, chunks):
        ups = [[tag() for _ in range(4)] for _ in chunks]
        downs = [[tag() for _ in range(4)] for _ in chunks]

        def step(j, z):
            below, above = chunk(lax.rem(y + 8 - j, 8), z), chunk(lax.rem(y + j, 8), z)
            last_up, last_down = chunks[z]
            if 0 < j < 4 or (j == 4 and last_up):
                landed(below, ups[z][j - 1])
            if 0 < j < 4 or (j == 4 and last_down):
                landed(above, downs[z][j - 1])
            if j < 3 or (j == 3 and last_up):
                send(below, below, ups[z][j], device_y(1))
            if j < 3 or (j == 3 and last_down):
                send(above, above, downs[z][j], device_y(7))

        return step

    rows_a, rows_b = pl.ds(0, 32), pl.ds(32, 32)
    a_x = ring_x(lambda xx, z: wf.at[z, xx, y, rows_a])
    a_y = ring_y(lambda yy, z: wf.at[z, :, yy, rows_a], ((True, False), (False, True)))
    b_y = ring_y(lambda yy, z: wf.at[z, x, yy, rows_b], ((True, False), (False, True)))
    b_x = ring_x(lambda xx, z: wf.at[z, xx, :, rows_b])

    f_up, f_down = tag(), tag()
    s_tags = {key: tag() for key in ("d0", "d1", "u0", "u1", "f0", "f1")}

    def pass_on():
        landed(hid.at[down, half(0)], h_up[0])
        send(hid.at[down, half(0)], hid.at[down, half(0)], f_up, (dp, up))
        landed(hid.at[up, half(1)], h_down[1])
        send(hid.at[up, half(1)], hid.at[up, half(1)], f_down, (dp, down))

    def to_sib(owner, q, key):
        send(hid.at[owner, half(q)], hid.at[owner, half(q)], s_tags[key], (dp, sib))

    landed(wf.at[1 - zl, x, y], w_z)
    b_y(0, 0)
    b_y(0, 1)
    a_x[0]()

    h_up, h_down = [tag() for _ in range(2)], [tag() for _ in range(2)]
    h_sib = tag()
    for q in range(2):
        send(h.at[half(q)], hid.at[mp, half(q)], h_up[q], (dp, up))
        send(h.at[half(1 - q)], hid.at[mp, half(1 - q)], h_down[1 - q], (dp, down))
    send(h, hid.at[mp], h_sib, (dp, sib))

    row_of = lax.broadcasted_iota(jnp.int32, (256, 1024), 0)
    col_of = lax.broadcasted_iota(jnp.int32, (256, 1024), 1)
    slot_of = ((lax.shift_right_logical(col_of, 4) * 4 + (col_of & 3)) == row_of).astype(F32).astype(BF16)
    numbers8 = jnp.broadcast_to(assign_row[...].astype(F32), (8, 256)).astype(BF16)
    number_of = mm(numbers8, slot_of)[0:1].astype(jnp.int32)
    one_hot[...] = (row_of == number_of).astype(F32).astype(BF16)

    b_y(1, 0)
    b_y(1, 1)
    a_x[1]()
    a_x[2]()
    a_y(0, 0)
    a_y(0, 1)
    collect(low_tags)
    low_full[mp] = jnp.sum(low_recv[...].astype(F32), axis=0).astype(BF16)
    low_all = spread("mp", lambda p: low_full.at[mp], low_full.at[mp], low_full.at[first7])
    b_y(2, 0)
    b_y(2, 1)
    collect(pos_y)
    pos_zx = spread("zx", lambda p: pb.at[zx], pb.at[zx], pb.at[first7])
    b_y(3, 0)
    b_y(3, 1)
    a_y(1, 0)
    b_y(4, 0)
    b_y(4, 1)
    b_x[0]()
    a_y(1, 1)
    a_y(2, 0)
    pass_on()
    b_x[1]()
    a_y(2, 1)
    to_sib(down, 0, "d0")
    to_sib(up, 1, "u1")
    landed(hid.at[down, half(1)], h_up[1])
    landed(hid.at[up, half(0)], h_down[0])
    to_sib(down, 1, "d1")
    to_sib(up, 0, "u0")
    a_y(3, 0)
    a_y(3, 1)

    def joined(ref):
        halves = [jnp.concatenate([ref[4 * r + t] for t in range(4)], axis=1) for r in range(2)]
        return jnp.concatenate(halves, axis=0)

    collect(low_all)
    collect(pos_zx)
    low = joined(low_full)
    low_rows = low.astype(F32).T.astype(BF16)
    acc[...] = adapter_factor_scale * mm(low_rows, b[...])
    landed(hid.at[sib], h_sib)
    b_x[2]()
    a_y(4, 0)
    a_y(4, 1)

    def slab(m):
        return wf[lax.div(m, 4), lax.rem(m, 4)].reshape(512, 512)

    def tokens(i):
        return pl.ds(pl.multiple_of(256 * i, 256), 256)

    @pl.loop(0, 2)
    def _(i):
        t = tokens(i)
        acc[t] += mm(h[t], slab(mp)) + mm(hid[sib, t], slab(sib))

    landed(hid.at[far, half(0)], f_up)
    to_sib(far, 0, "f0")
    landed(hid.at[far, half(1)], f_down)
    to_sib(far, 1, "f1")
    landed(hid.at[sib_down, half(0)], s_tags["d0"])
    landed(hid.at[sib_up, half(1)], s_tags["u1"])
    landed(hid.at[sib_down, half(1)], s_tags["d1"])
    landed(hid.at[sib_up, half(0)], s_tags["u0"])

    @pl.loop(0, 2)
    def _(i):
        t = tokens(i)
        total = acc[t]
        for m in (down, up, sib_down, sib_up):
            total += mm(hid[m, t], slab(m))
        acc[t] = total

    landed(hid.at[sib_far, half(0)], s_tags["f0"])
    landed(hid.at[sib_far, half(1)], s_tags["f1"])

    ones = jnp.ones((8, 128), BF16)

    @pl.loop(0, 2)
    def _(i):
        t = tokens(i)
        total = acc[t] + h[t].astype(F32)
        for m in (far, sib_far):
            total += mm(hid[m, t], slab(m))
        pre[t] = total.astype(BF16)
        squares = total * total
        squares = squares[:, 0:128] + squares[:, 128:256] + squares[:, 256:384] + squares[:, 384:512]
        high = squares.astype(BF16)
        rest = (squares - high.astype(F32)).astype(BF16)
        sq_row[i] = mm(ones, high, NT) + mm(ones, rest, NT)

    row8 = lax.broadcasted_iota(jnp.int32, (8, 128), 0)
    lane8 = lax.broadcasted_iota(jnp.int32, (8, 128), 1)

    def by_sequence(wide):
        value = jnp.zeros((8, 128), F32)
        for s in range(4):
            value = jnp.where(lax.rem(row8, 4) == s, wide[:, 128 * s : 128 * s + 128], value)
        return value

    def diagonal(value, first, every):
        keep = lax.rem(row8, 4) if every else row8 - first
        return jnp.concatenate([jnp.where(keep == s, value, 0.0) for s in range(4)], axis=1)

    sq[mp] = by_sequence(jnp.concatenate([sq_row[0], sq_row[1]], axis=1))
    sq_tags = spread("mp", lambda p: sq.at[mp], sq.at[mp], sq.at[first7])

    p_t = mm(b[...], pre[...], NT)
    for o in range(8):
        p_part[o] = p_t[16 * (o // 4) : 16 * (o // 4) + 16, 128 * (o % 4) : 128 * (o % 4) + 128].astype(BF16)
    p_tags = spread("mp", lambda p: p_part.at[p], p_recv.at[mp], p_recv.at[first7])
    p_recv[mp] = p_part[mp]

    lengths = jnp.zeros((8, 128), jnp.int32)
    mine = jnp.zeros((8, 256), jnp.int32)
    row256 = lax.broadcasted_iota(jnp.int32, (8, 256), 0)
    lane256 = lax.broadcasted_iota(jnp.int32, (8, 256), 1)
    for s in range(4):
        number = assign[dp * 4 + s]
        lengths = jnp.where(lax.rem(row8, 4) == s, counts[number], lengths)
        mine = jnp.where(lax.rem(row256, 4) == s, number, mine)
    weight = jnp.where(lane8 < lengths, 1.0, 0.0) / lengths.astype(F32)

    collect(sq_tags)
    inv_rms = lax.rsqrt(jnp.sum(sq[...], axis=0) / WIDTH + 1e-05)
    alpha = weight * inv_rms
    mean = mm_split(diagonal(alpha, 0, True), pre[...])
    tile = [
        jnp.where(row8 < 4, mean[:, 256 * j : 256 * j + 128], mean[:, 256 * j + 128 : 256 * j + 256])
        for j in range(2)
    ]
    pooled[zx, y] = jnp.concatenate(tile, axis=0).astype(BF16)

    y_tags = spread("y", lambda p: pooled.at[zx, y], pooled.at[zx, y], pooled.at[zx, first7])
    collect(p_tags)
    p_full[mp] = jnp.sum(p_recv[...].astype(F32), axis=0).astype(BF16)
    p_all = spread("mp", lambda p: p_full.at[mp], p_full.at[mp], p_full.at[first7])
    collect(y_tags)
    zx_tags = spread("zx", lambda p: pooled.at[zx], pooled.at[zx], pooled.at[first7])
    collect(zx_tags)
    gathered = pooled[...].reshape(1024, 128)
    quarter = lax.shift_right_logical(lax.broadcasted_iota(jnp.int32, (1024, 128), 0), 2) & 3
    for j in range(4):
        chosen = jnp.where(quarter == j, gathered.astype(F32), 0.0).astype(BF16)
        units[:, 128 * j : 128 * j + 128] = mm(one_hot[...], chosen).astype(BF16)

    x_part[...] = mm(units[0:64], units[...], NT).reshape(8, 8, 256)
    x_tags = spread("mp", lambda p: x_part.at[p], x_recv.at[mp], x_recv.at[first7])
    square = units[...].astype(F32)
    square = square * square
    high = square.astype(BF16)
    rest = (square - high.astype(F32)).astype(BF16)
    ones_wide = jnp.ones((8, 512), BF16)
    n_recv[mp] = (mm(ones_wide, high, NT) + mm(ones_wide, rest, NT))[0:1]
    n_tags = spread("mp", lambda p: n_recv.at[mp], n_recv.at[mp], n_recv.at[first7])
    x_recv[mp] = x_part[mp]
    collect(x_tags)
    x_full[mp] = jnp.sum(x_recv[...], axis=0)
    g_tags = spread("mp", lambda p: x_full.at[mp], x_full.at[mp], x_full.at[first7])
    collect(n_tags)
    lengths_sq = n_recv[0]
    for s in range(1, 8):
        lengths_sq = lengths_sq + n_recv[s]
    inv_norm = 1.0 / jnp.sqrt(lengths_sq + 1e-06)
    rowq = lax.broadcasted_iota(jnp.int32, (64, 256), 0)
    laneq = lax.broadcasted_iota(jnp.int32, (64, 256), 1)
    inv_query = jnp.sum(jnp.where(rowq == laneq, inv_norm, 0.0), axis=1, keepdims=True)
    scale = score_scale * inv_query * inv_norm
    document = laneq >= 64
    positive = pb[...].reshape(64, 1, 128)[:, 0, :]
    positive = jnp.concatenate([positive, positive], axis=1)
    positive_mask = jnp.where((laneq - 64).astype(F32) == positive, 1.0, 0.0)
    collect(g_tags)

    scores = jnp.where(document, scale * x_full[...].reshape(64, 256), 0.0)
    exponents = jnp.where(document, jnp.exp(scores), 0.0)
    exp_total = jnp.sum(exponents, axis=1, keepdims=True)
    query_loss = jnp.log(exp_total) - jnp.sum(positive_mask * scores, axis=1, keepdims=True)
    loss[0] = jnp.sum(jnp.where(rowq[:, 0:1] == dp, query_loss, 0.0))
    score_grads = exponents / exp_total - positive_mask
    inner = score_grads * scores
    inner_query = jnp.sum(inner, axis=1, keepdims=True)
    inner_document = jnp.sum(inner, axis=0, keepdims=True)
    coef = scale * score_grads

    below = jnp.zeros((192, 256), F32)
    coef_query = coef - jnp.where(rowq == laneq, inner_query * inv_query * inv_query, 0.0)
    own = (lane256 == mine).astype(F32)
    own_document = jnp.where(lane256 >= 64, own, 0.0)

    def picked(rows, matrix, dims):
        matrix = jnp.concatenate([matrix, below], axis=0)
        top = matrix.astype(BF16)
        return mm(rows, top, dims) + mm(rows, (matrix - top.astype(F32)).astype(BF16), dims)

    mix = (
        picked(own.astype(BF16), coef_query, NN)
        + picked(own_document.astype(BF16), coef, NT)
        - own_document * (inner_document * inv_norm * inv_norm)
    )
    grad = mm_split(mix, units[...])

    b_wide = jnp.concatenate([b[...].astype(F32), jnp.zeros((96, 512), F32)], axis=0).astype(BF16)
    ex[mp] = jnp.where(row8 < 4, by_sequence(mm_split(grad, pre[...], NT)), mm_split(grad, b_wide, NT))
    e_tags = spread("mp", lambda p: ex.at[mp], ex.at[mp], ex.at[first7])
    alpha_top, alpha_low = diagonal(alpha, 0, False), diagonal(alpha, 4, False)
    low_grad = mm_exact(mm_exact(low.astype(F32), alpha_top, NT), grad)
    collect(p_all)
    p_rows = joined(p_full).astype(F32)
    collect(e_tags)
    total = jnp.sum(ex[...], axis=0)
    beta = inv_rms * inv_rms * alpha * total / WIDTH
    beta_row = jnp.sum(diagonal(beta, 0, False), axis=0, keepdims=True)
    up_grad = mm_exact(total.T[0:32], alpha_low)
    grad_low = (adapter_factor_scale * (up_grad - p_rows * beta_row)).astype(BF16)
    part_a = mm(grad_low, h[...])
    part_b = adapter_factor_scale * (low_grad - mm((low.astype(F32) * beta_row).astype(BF16), pre[...]))

    f_part[0:4] = part_a.reshape(4, 8, 512)
    f_part[4:8] = part_b.reshape(4, 8, 512)
    tags1 = spread("zx", lambda p: f_part.at[p], f_recv.at[zx], f_recv.at[first7])
    f_recv[zx] = f_part[zx]
    collect(tags1)
    f_mid[y] = jnp.sum(f_recv[...], axis=0)
    tags2 = spread("y", lambda p: f_mid.at[y], f_mid.at[y], f_mid.at[first7])
    collect(tags2)
    f_out[zx] = jnp.sum(f_mid[...], axis=0)
    tags3 = spread("zx", lambda p: f_out.at[zx], f_out.at[zx], f_out.at[first7])
    collect(tags3)
    grad_a[...] = f_out[0:4].reshape(32, 512)
    grad_b[...] = f_out[4:8].reshape(32, 512)

    for copy in started:
        copy.wait_send()
    assert used[0] == TAGS, used[0]


def body(hidden, frozen_matrix, adapter_down_weight, adapter_up_weight, sequence_token_counts, assignment, positives):
    vmem, smem = pl.BlockSpec(memory_space=pltpu.VMEM), pl.BlockSpec(memory_space=pltpu.SMEM)
    anywhere = pl.BlockSpec(memory_space=pltpu.HBM)
    V = pltpu.VMEM
    loss, grad_a, grad_b = pl.pallas_call(
        kernel,
        out_shape=(
            jax.ShapeDtypeStruct((1,), F32),
            jax.ShapeDtypeStruct((32, 512), F32),
            jax.ShapeDtypeStruct((32, 512), F32),
        ),
        in_specs=[anywhere, anywhere, anywhere, anywhere, smem, smem, smem, vmem],
        out_specs=(smem, vmem, vmem),
        scratch_shapes=[
            V((512, 512), BF16),
            V((64, 512), BF16),
            V((32, 512), BF16),
            V((32, 512), BF16),
            V((8, 512, 512), BF16),
            V((2, 4, 8, 64, 512), BF16),
            V((8, 16, 128), BF16),
            V((8, 16, 128), BF16),
            V((8, 16, 128), BF16),
            V((8, 8, 1, 128), F32),
            V((512, 512), F32),
            V((512, 512), BF16),
            V((2, 8, 256), F32),
            V((256, 1024), BF16),
            V((8, 8, 128), F32),
            V((8, 16, 128), BF16),
            V((8, 16, 128), BF16),
            V((8, 16, 128), BF16),
            V((8, 8, 16, 128), BF16),
            V((256, 512), BF16),
            V((8, 8, 256), F32),
            V((8, 8, 256), F32),
            V((8, 8, 256), F32),
            V((8, 1, 256), F32),
            V((8, 8, 128), F32),
            V((8, 8, 512), F32),
            V((8, 8, 512), F32),
            V((8, 8, 512), F32),
            V((8, 8, 512), F32),
            pltpu.SemaphoreType.DMA((TAGS,)),
            pltpu.SemaphoreType.DMA((TAGS,)),
            pltpu.SemaphoreType.DMA((4,)),
        ],
        compiler_params=pltpu.CompilerParams(
            collective_id=0, has_side_effects=True, vmem_limit_bytes=48 * 1024 * 1024
        ),
    )(
        hidden.reshape(512, 512),
        frozen_matrix,
        adapter_down_weight.T,
        adapter_up_weight,
        positives,
        sequence_token_counts,
        assignment,
        assignment.reshape(1, 256),
    )
    return loss, grad_a.T, grad_b


def solution(mesh):
    return jax.shard_map(
        body,
        mesh=mesh,
        in_specs=(
            P("dp", None, "mp"),
            P("dp", "mp"),
            P("mp", None),
            P(None, "mp"),
            P(),
            P(),
            P("dp"),
        ),
        out_specs=(P("dp"), P("mp", None), P(None, "mp")),
        check_vma=False,
    )
```

```python
import jax
import jax.numpy as jnp
from jax import lax
from jax.experimental import pallas as pl
from jax.experimental.pallas import tpu as pltpu
from jax.sharding import PartitionSpec as P

MESH = pl.DeviceIdType.MESH
F32, BF16 = jnp.float32, jnp.bfloat16
score_scale = 20.0
adapter_factor_scale = 2.0
WIDTH = 4096
TAGS = 74

NN = (((1,), (0,)), ((), ()))
NT = (((1,), (1,)), ((), ()))


def mm(left, right, dims=NN):
    return lax.dot_general(left, right, dims, preferred_element_type=F32)


def mm_exact(left, right, dims=NN):
    return lax.dot_general(left, right, dims, precision=lax.Precision.HIGHEST, preferred_element_type=F32)


def split_rows(value):
    high = value.astype(BF16).astype(F32)
    return jnp.concatenate([high, value - high], axis=0).astype(BF16)


def mm_split(value, right, dims=NN):
    rows = value.shape[0]
    both = mm(split_rows(value), right, dims)
    return both[:rows] + both[rows:]


def kernel(
    h_in, w_in, a_in, b_in, pos, counts, assign, assign_row,
    loss, grad_a, grad_b,
    h, w, a, b, hid, wf, low_part, low_recv, low_full, pb,
    acc, pre, sq_row, one_hot, sq, p_part, p_recv, p_full,
    pooled, units, x_part, x_recv, x_full, n_recv, ex,
    f_part, f_recv, f_mid, f_out,
    send_sem, recv_sem, load_sem,
):
    dp, mp = lax.axis_index("dp"), lax.axis_index("mp")
    y = lax.rem(dp, 8)
    zx = lax.div(dp, 8)
    zl, x = lax.div(zx, 4), lax.rem(zx, 4)
    zh, core = lax.div(mp, 2), lax.rem(mp, 2)
    sib = zh * 2 + 1 - core
    up, down = lax.rem(zh + 1, 4) * 2 + core, lax.rem(zh + 3, 4) * 2 + core
    far = lax.rem(zh + 2, 4) * 2 + core
    sib_up, sib_down = lax.rem(zh + 1, 4) * 2 + 1 - core, lax.rem(zh + 3, 4) * 2 + 1 - core
    sib_far = lax.rem(zh + 2, 4) * 2 + 1 - core

    index_of = {"mp": mp, "y": y, "zx": zx}
    device_of = {
        "mp": lambda p: (dp, p),
        "y": lambda p: (zx * 8 + p, mp),
        "zx": lambda p: (p * 8 + y, mp),
    }
    used = [0]
    started = []

    def tag():
        used[0] += 1
        return used[0] - 1

    def remote(src, dst, number, device):
        return pltpu.make_async_remote_copy(
            src_ref=src, dst_ref=dst, send_sem=send_sem.at[number], recv_sem=recv_sem.at[number],
            device_id=device, device_id_type=MESH,
        )

    def send(src, dst, number, device):
        copy = remote(src, dst, number, device)
        copy.start()
        started.append(copy)

    def landed(region, number):
        remote(region, region, number, (dp, sib)).wait_recv()

    def spread(kind, src, dst, seven):
        me, number = index_of[kind], tag()
        for k in range(1, 8):
            peer = lax.rem(me + k, 8)
            remote(src(peer), dst, number, device_of[kind](peer)).start()
        started.append(remote(seven, seven, number, (dp, sib)))
        return number, seven

    def collect(ticket):
        landed(ticket[1], ticket[0])

    loads = [
        pltpu.make_async_copy(src, dst, load_sem.at[i])
        for i, (src, dst) in enumerate(((w_in, w), (h_in, h), (a_in, a), (b_in, b)))
    ]

    barrier = pltpu.get_barrier_semaphore()
    for kind in ("mp", "y", "zx"):
        for k in range(1, 8):
            pl.semaphore_signal(barrier, inc=1, device_id=device_of[kind](lax.rem(index_of[kind] + k, 8)), device_id_type=MESH)
    for copy in loads:
        copy.start()
    pb[zx, y] = jnp.full((1, 128), pos[0].astype(F32), F32)
    first7 = pl.ds(0, 7)
    loads[0].wait()
    wf[zl, x, y] = w[...]
    for copy in loads[1:]:
        copy.wait()
    low_t = mm(a[...], h[...], NT)
    for o in range(8):
        low_part[o] = low_t[16 * (o // 4) : 16 * (o // 4) + 16, 128 * (o % 4) : 128 * (o % 4) + 128].astype(BF16)
    low_recv[mp] = low_part[mp]
    pl.semaphore_wait(barrier, 21)

    w_z = tag()
    send(w, wf.at[zl, x, y], w_z, ((1 - zl) * 32 + x * 8 + y, mp))

    low_tags = spread("mp", lambda p: low_part.at[p], low_recv.at[mp], low_recv.at[first7])

    def half(q):
        return pl.ds(256 * q, 256)

    pos_y = spread("y", lambda p: pb.at[zx, y], pb.at[zx, y], pb.at[zx, first7])

    def device_x(k):
        return (zl * 32 + lax.rem(x + k, 4) * 8 + y, mp)

    def device_y(k):
        return (zx * 8 + lax.rem(y + k, 8), mp)

    def ring_x(view):
        tags = [tag() for _ in range(6)]
        before, after, across = lax.rem(x + 3, 4), lax.rem(x + 1, 4), lax.rem(x + 2, 4)

        def first(z):
            send(view(x, z), view(x, z), tags[(0, 2)[z]], device_x(1))
            send(view(x, z), view(x, z), tags[(3, 1)[z]], device_x(3))

        def second():
            landed(view(before, 0), tags[0])
            send(view(before, 0), view(before, 0), tags[4], device_x(1))
            landed(view(after, 1), tags[1])
            send(view(after, 1), view(after, 1), tags[5], device_x(3))

        def last():
            landed(view(before, 1), tags[2])
            landed(view(after, 0), tags[3])
            landed(view(across, 0), tags[4])
            landed(view(across, 1), tags[5])

        return first, second, last

    def ring_y(chunk, chunks):
        ups = [[tag() for _ in range(4)] for _ in chunks]
        downs = [[tag() for _ in range(4)] for _ in chunks]

        def step(j, z):
            below, above = chunk(lax.rem(y + 8 - j, 8), z), chunk(lax.rem(y + j, 8), z)
            last_up, last_down = chunks[z]
            if 0 < j < 4 or (j == 4 and last_up):
                landed(below, ups[z][j - 1])
            if 0 < j < 4 or (j == 4 and last_down):
                landed(above, downs[z][j - 1])
            if j < 3 or (j == 3 and last_up):
                send(below, below, ups[z][j], device_y(1))
            if j < 3 or (j == 3 and last_down):
                send(above, above, downs[z][j], device_y(7))

        return step

    rows_a, rows_b = pl.ds(0, 32), pl.ds(32, 32)
    plane = (zl, 1 - zl)
    a_x = ring_x(lambda xx, z: wf.at[plane[z], xx, y, rows_a])
    a_y = ring_y(lambda yy, z: wf.at[plane[z], :, yy, rows_a], ((True, False), (False, True)))
    b_y = ring_y(lambda yy, z: wf.at[plane[z], x, yy, rows_b], ((True, False), (False, True)))
    b_x = ring_x(lambda xx, z: wf.at[plane[z], xx, :, rows_b])

    f_up, f_down = tag(), tag()
    s_tags = {key: tag() for key in ("d0", "d1", "u0", "u1", "f0", "f1")}

    def pass_on():
        landed(hid.at[down, half(0)], h_up[0])
        send(hid.at[down, half(0)], hid.at[down, half(0)], f_up, (dp, up))
        landed(hid.at[up, half(1)], h_down[1])
        send(hid.at[up, half(1)], hid.at[up, half(1)], f_down, (dp, down))

    def to_sib(owner, q, key):
        send(hid.at[owner, half(q)], hid.at[owner, half(q)], s_tags[key], (dp, sib))

    a_x[0](0)
    b_y(0, 0)
    landed(wf.at[1 - zl, x, y], w_z)
    a_x[0](1)
    b_y(0, 1)

    h_up, h_down = [tag() for _ in range(2)], [tag() for _ in range(2)]
    h_sib = tag()
    for q in range(2):
        send(h.at[half(q)], hid.at[mp, half(q)], h_up[q], (dp, up))
        send(h.at[half(1 - q)], hid.at[mp, half(1 - q)], h_down[1 - q], (dp, down))
    send(h, hid.at[mp], h_sib, (dp, sib))

    row_of = lax.broadcasted_iota(jnp.int32, (256, 1024), 0)
    col_of = lax.broadcasted_iota(jnp.int32, (256, 1024), 1)
    slot_of = ((lax.shift_right_logical(col_of, 4) * 4 + (col_of & 3)) == row_of).astype(F32).astype(BF16)
    numbers8 = jnp.broadcast_to(assign_row[...].astype(F32), (8, 256)).astype(BF16)
    number_of = mm(numbers8, slot_of)[0:1].astype(jnp.int32)
    one_hot[...] = (row_of == number_of).astype(F32).astype(BF16)

    b_y(1, 0)
    b_y(1, 1)
    a_x[1]()
    a_x[2]()
    a_y(0, 0)
    a_y(0, 1)
    collect(low_tags)
    low_full[mp] = jnp.sum(low_recv[...].astype(F32), axis=0).astype(BF16)
    low_all = spread("mp", lambda p: low_full.at[mp], low_full.at[mp], low_full.at[first7])
    b_y(2, 0)
    b_y(2, 1)
    collect(pos_y)
    pos_zx = spread("zx", lambda p: pb.at[zx], pb.at[zx], pb.at[first7])
    b_y(3, 0)
    b_y(3, 1)
    a_y(1, 0)
    b_y(4, 0)
    b_y(4, 1)
    b_x[0](0)
    b_x[0](1)
    a_y(1, 1)
    a_y(2, 0)
    pass_on()
    b_x[1]()
    a_y(2, 1)
    to_sib(down, 0, "d0")
    to_sib(up, 1, "u1")
    landed(hid.at[down, half(1)], h_up[1])
    landed(hid.at[up, half(0)], h_down[0])
    to_sib(down, 1, "d1")
    to_sib(up, 0, "u0")
    a_y(3, 0)
    a_y(3, 1)

    def joined(ref):
        halves = [jnp.concatenate([ref[4 * r + t] for t in range(4)], axis=1) for r in range(2)]
        return jnp.concatenate(halves, axis=0)

    collect(low_all)
    collect(pos_zx)
    low = joined(low_full)
    low_rows = low.astype(F32).T.astype(BF16)
    acc[...] = adapter_factor_scale * mm(low_rows, b[...])
    landed(hid.at[sib], h_sib)
    b_x[2]()
    a_y(4, 0)
    a_y(4, 1)

    def slab(m):
        return wf[lax.div(m, 4), lax.rem(m, 4)].reshape(512, 512)

    def tokens(i):
        return pl.ds(pl.multiple_of(256 * i, 256), 256)

    @pl.loop(0, 2)
    def _(i):
        t = tokens(i)
        acc[t] += mm(h[t], slab(mp)) + mm(hid[sib, t], slab(sib))

    landed(hid.at[far, half(0)], f_up)
    to_sib(far, 0, "f0")
    landed(hid.at[far, half(1)], f_down)
    to_sib(far, 1, "f1")
    landed(hid.at[sib_down, half(0)], s_tags["d0"])
    landed(hid.at[sib_up, half(1)], s_tags["u1"])
    landed(hid.at[sib_down, half(1)], s_tags["d1"])
    landed(hid.at[sib_up, half(0)], s_tags["u0"])

    @pl.loop(0, 2)
    def _(i):
        t = tokens(i)
        total = acc[t]
        for m in (down, up, sib_down, sib_up):
            total += mm(hid[m, t], slab(m))
        acc[t] = total

    landed(hid.at[sib_far, half(0)], s_tags["f0"])
    landed(hid.at[sib_far, half(1)], s_tags["f1"])

    ones = jnp.ones((8, 128), BF16)

    @pl.loop(0, 2)
    def _(i):
        t = tokens(i)
        total = acc[t] + h[t].astype(F32)
        for m in (far, sib_far):
            total += mm(hid[m, t], slab(m))
        pre[t] = total.astype(BF16)
        squares = total * total
        squares = squares[:, 0:128] + squares[:, 128:256] + squares[:, 256:384] + squares[:, 384:512]
        high = squares.astype(BF16)
        rest = (squares - high.astype(F32)).astype(BF16)
        sq_row[i] = mm(ones, high, NT) + mm(ones, rest, NT)

    row8 = lax.broadcasted_iota(jnp.int32, (8, 128), 0)
    lane8 = lax.broadcasted_iota(jnp.int32, (8, 128), 1)

    def by_sequence(wide):
        value = jnp.zeros((8, 128), F32)
        for s in range(4):
            value = jnp.where(lax.rem(row8, 4) == s, wide[:, 128 * s : 128 * s + 128], value)
        return value

    def diagonal(value, first, every):
        keep = lax.rem(row8, 4) if every else row8 - first
        return jnp.concatenate([jnp.where(keep == s, value, 0.0) for s in range(4)], axis=1)

    sq[mp] = by_sequence(jnp.concatenate([sq_row[0], sq_row[1]], axis=1))
    sq_tags = spread("mp", lambda p: sq.at[mp], sq.at[mp], sq.at[first7])

    p_t = mm(b[...], pre[...], NT)
    for o in range(8):
        p_part[o] = p_t[16 * (o // 4) : 16 * (o // 4) + 16, 128 * (o % 4) : 128 * (o % 4) + 128].astype(BF16)
    p_tags = spread("mp", lambda p: p_part.at[p], p_recv.at[mp], p_recv.at[first7])
    p_recv[mp] = p_part[mp]

    lengths = jnp.zeros((8, 128), jnp.int32)
    mine = jnp.zeros((8, 256), jnp.int32)
    row256 = lax.broadcasted_iota(jnp.int32, (8, 256), 0)
    lane256 = lax.broadcasted_iota(jnp.int32, (8, 256), 1)
    for s in range(4):
        number = assign[dp * 4 + s]
        lengths = jnp.where(lax.rem(row8, 4) == s, counts[number], lengths)
        mine = jnp.where(lax.rem(row256, 4) == s, number, mine)
    weight = jnp.where(lane8 < lengths, 1.0, 0.0) / lengths.astype(F32)

    collect(sq_tags)
    inv_rms = lax.rsqrt(jnp.sum(sq[...], axis=0) / WIDTH + 1e-05)
    alpha = weight * inv_rms
    mean = mm_split(diagonal(alpha, 0, True), pre[...])
    tile = [
        jnp.where(row8 < 4, mean[:, 256 * j : 256 * j + 128], mean[:, 256 * j + 128 : 256 * j + 256])
        for j in range(2)
    ]
    pooled[zx, y] = jnp.concatenate(tile, axis=0).astype(BF16)

    y_tags = spread("y", lambda p: pooled.at[zx, y], pooled.at[zx, y], pooled.at[zx, first7])
    collect(p_tags)
    p_full[mp] = jnp.sum(p_recv[...].astype(F32), axis=0).astype(BF16)
    p_all = spread("mp", lambda p: p_full.at[mp], p_full.at[mp], p_full.at[first7])
    collect(y_tags)
    zx_tags = spread("zx", lambda p: pooled.at[zx], pooled.at[zx], pooled.at[first7])
    collect(zx_tags)
    row16 = lax.shift_right_logical(lax.broadcasted_iota(jnp.int32, (16, 128), 0), 2)
    gathered = pooled[...].reshape(64, 16, 128)
    chosen = [(gathered * (row16 == j).astype(F32).astype(BF16)[None]).reshape(1024, 128) for j in range(4)]
    units[...] = mm(one_hot[...], jnp.concatenate(chosen, axis=1)).astype(BF16)

    x_part[...] = mm(units[0:64], units[...], NT).reshape(8, 8, 256)
    x_tags = spread("mp", lambda p: x_part.at[p], x_recv.at[mp], x_recv.at[first7])
    square = units[...].astype(F32)
    square = square * square
    high = square.astype(BF16)
    rest = (square - high.astype(F32)).astype(BF16)
    ones_wide = jnp.ones((8, 512), BF16)
    n_recv[mp] = (mm(ones_wide, high, NT) + mm(ones_wide, rest, NT))[0:1]
    n_tags = spread("mp", lambda p: n_recv.at[mp], n_recv.at[mp], n_recv.at[first7])
    x_recv[mp] = x_part[mp]
    collect(x_tags)
    x_full[mp] = jnp.sum(x_recv[...], axis=0)
    g_tags = spread("mp", lambda p: x_full.at[mp], x_full.at[mp], x_full.at[first7])
    collect(n_tags)
    lengths_sq = n_recv[0]
    for s in range(1, 8):
        lengths_sq = lengths_sq + n_recv[s]
    inv_norm = 1.0 / jnp.sqrt(lengths_sq + 1e-06)
    rowq = lax.broadcasted_iota(jnp.int32, (64, 256), 0)
    laneq = lax.broadcasted_iota(jnp.int32, (64, 256), 1)
    inv_query = jnp.sum(jnp.where(rowq == laneq, inv_norm, 0.0), axis=1, keepdims=True)
    scale = score_scale * inv_query * inv_norm
    document = laneq >= 64
    positive = pb[...].reshape(64, 1, 128)[:, 0, :]
    positive = jnp.concatenate([positive, positive], axis=1)
    positive_mask = jnp.where((laneq - 64).astype(F32) == positive, 1.0, 0.0)
    collect(g_tags)

    scores = jnp.where(document, scale * x_full[...].reshape(64, 256), 0.0)
    exponents = jnp.where(document, jnp.exp(scores), 0.0)
    exp_total = jnp.sum(exponents, axis=1, keepdims=True)
    query_loss = jnp.log(exp_total) - jnp.sum(positive_mask * scores, axis=1, keepdims=True)
    loss[0] = jnp.sum(jnp.where(rowq[:, 0:1] == dp, query_loss, 0.0))
    score_grads = exponents / exp_total - positive_mask
    inner = score_grads * scores
    inner_query = jnp.sum(inner, axis=1, keepdims=True)
    inner_document = jnp.sum(inner, axis=0, keepdims=True)
    coef = scale * score_grads

    below = jnp.zeros((192, 256), F32)
    coef_query = coef - jnp.where(rowq == laneq, inner_query * inv_query * inv_query, 0.0)
    own = (lane256 == mine).astype(F32)
    own_document = jnp.where(lane256 >= 64, own, 0.0)

    def picked(rows, matrix, dims):
        matrix = jnp.concatenate([matrix, below], axis=0)
        top = matrix.astype(BF16)
        return mm(rows, top, dims) + mm(rows, (matrix - top.astype(F32)).astype(BF16), dims)

    mix = (
        picked(own.astype(BF16), coef_query, NN)
        + picked(own_document.astype(BF16), coef, NT)
        - own_document * (inner_document * inv_norm * inv_norm)
    )
    grad = mm_split(mix, units[...])

    b_wide = jnp.concatenate([b[...].astype(F32), jnp.zeros((96, 512), F32)], axis=0).astype(BF16)
    ex[mp] = jnp.where(row8 < 4, by_sequence(mm_split(grad, pre[...], NT)), mm_split(grad, b_wide, NT))
    e_tags = spread("mp", lambda p: ex.at[mp], ex.at[mp], ex.at[first7])
    alpha_top, alpha_low = diagonal(alpha, 0, False), diagonal(alpha, 4, False)
    low_grad = mm_exact(mm_exact(low.astype(F32), alpha_top, NT), grad)
    collect(p_all)
    p_rows = joined(p_full).astype(F32)
    collect(e_tags)
    total = jnp.sum(ex[...], axis=0)
    beta = inv_rms * inv_rms * alpha * total / WIDTH
    beta_row = jnp.sum(diagonal(beta, 0, False), axis=0, keepdims=True)
    up_grad = mm_exact(total.T[0:32], alpha_low)
    grad_low = (adapter_factor_scale * (up_grad - p_rows * beta_row)).astype(BF16)
    part_a = mm(grad_low, h[...])
    part_b = adapter_factor_scale * (low_grad - mm((low.astype(F32) * beta_row).astype(BF16), pre[...]))

    total = jnp.concatenate([part_a, part_b], axis=0).astype(BF16)
    for o in range(8):
        f_part[o] = total[16 * (o // 2) : 16 * (o // 2) + 16, 256 * (o % 2) : 256 * (o % 2) + 256]
    tags1 = spread("zx", lambda p: f_part.at[p], f_recv.at[zx], f_recv.at[first7])
    f_recv[zx] = f_part[zx]
    collect(tags1)
    f_mid[y] = jnp.sum(f_recv[...].astype(F32), axis=0).astype(BF16)
    tags2 = spread("y", lambda p: f_mid.at[y], f_mid.at[y], f_mid.at[first7])
    collect(tags2)
    f_out[zx] = jnp.sum(f_mid[...].astype(F32), axis=0).astype(BF16)
    tags3 = spread("zx", lambda p: f_out.at[zx], f_out.at[zx], f_out.at[first7])
    collect(tags3)
    for o in range(8):
        place = pl.ds(16 * (o // 2 % 2), 16), pl.ds(256 * (o % 2), 256)
        (grad_a if o < 4 else grad_b)[place] = f_out[o].astype(F32)

    for copy in started:
        copy.wait_send()
    assert used[0] == TAGS, used[0]


def body(hidden, frozen_matrix, adapter_down_weight, adapter_up_weight, sequence_token_counts, assignment, positives):
    vmem, smem = pl.BlockSpec(memory_space=pltpu.VMEM), pl.BlockSpec(memory_space=pltpu.SMEM)
    anywhere = pl.BlockSpec(memory_space=pltpu.HBM)
    V = pltpu.VMEM
    loss, grad_a, grad_b = pl.pallas_call(
        kernel,
        out_shape=(
            jax.ShapeDtypeStruct((1,), F32),
            jax.ShapeDtypeStruct((32, 512), F32),
            jax.ShapeDtypeStruct((32, 512), F32),
        ),
        in_specs=[anywhere, anywhere, anywhere, anywhere, smem, smem, smem, vmem],
        out_specs=(smem, vmem, vmem),
        scratch_shapes=[
            V((512, 512), BF16),
            V((64, 512), BF16),
            V((32, 512), BF16),
            V((32, 512), BF16),
            V((8, 512, 512), BF16),
            V((2, 4, 8, 64, 512), BF16),
            V((8, 16, 128), BF16),
            V((8, 16, 128), BF16),
            V((8, 16, 128), BF16),
            V((8, 8, 1, 128), F32),
            V((512, 512), F32),
            V((512, 512), BF16),
            V((2, 8, 256), F32),
            V((256, 1024), BF16),
            V((8, 8, 128), F32),
            V((8, 16, 128), BF16),
            V((8, 16, 128), BF16),
            V((8, 16, 128), BF16),
            V((8, 8, 16, 128), BF16),
            V((256, 512), BF16),
            V((8, 8, 256), F32),
            V((8, 8, 256), F32),
            V((8, 8, 256), F32),
            V((8, 1, 256), F32),
            V((8, 8, 128), F32),
            V((8, 16, 256), BF16),
            V((8, 16, 256), BF16),
            V((8, 16, 256), BF16),
            V((8, 16, 256), BF16),
            pltpu.SemaphoreType.DMA((TAGS,)),
            pltpu.SemaphoreType.DMA((TAGS,)),
            pltpu.SemaphoreType.DMA((4,)),
        ],
        compiler_params=pltpu.CompilerParams(
            collective_id=0, has_side_effects=True, vmem_limit_bytes=60 * 1024 * 1024
        ),
    )(
        hidden.reshape(512, 512),
        frozen_matrix,
        adapter_down_weight.T,
        adapter_up_weight,
        positives,
        sequence_token_counts,
        assignment,
        assignment.reshape(1, 256),
    )
    return loss, grad_a.T, grad_b


def solution(mesh):
    return jax.shard_map(
        body,
        mesh=mesh,
        in_specs=(
            P("dp", None, "mp"),
            P("dp", "mp"),
            P("mp", None),
            P(None, "mp"),
            P(),
            P(),
            P("dp"),
        ),
        out_specs=(P("dp"), P("mp", None), P(None, "mp")),
        check_vma=False,
    )
```

```python
import jax
import jax.numpy as jnp
from jax import lax
from jax.experimental import pallas as pl
from jax.experimental.pallas import tpu as pltpu
from jax.sharding import PartitionSpec as P

MESH = pl.DeviceIdType.MESH
F32, BF16 = jnp.float32, jnp.bfloat16
score_scale = 20.0
adapter_factor_scale = 2.0
WIDTH = 4096
TAGS = 74

NN = (((1,), (0,)), ((), ()))
NT = (((1,), (1,)), ((), ()))


def mm(left, right, dims=NN):
    return lax.dot_general(left, right, dims, preferred_element_type=F32)


def mm_exact(left, right, dims=NN):
    return lax.dot_general(left, right, dims, precision=lax.Precision.HIGHEST, preferred_element_type=F32)


def split_rows(value):
    high = value.astype(BF16).astype(F32)
    return jnp.concatenate([high, value - high], axis=0).astype(BF16)


def mm_split(value, right, dims=NN):
    rows = value.shape[0]
    both = mm(split_rows(value), right, dims)
    return both[:rows] + both[rows:]


def kernel(
    h_in, w_in, a_in, b_in, pos, counts, assign, assign_row,
    loss, grad_a, grad_b,
    h, w, a, b, hid, wf, low_part, low_recv, low_full, pb,
    acc, pre, sq_row, one_hot, sq, p_part, p_recv, p_full,
    pooled, units, x_part, x_recv, x_full, n_recv, ex,
    f_part, f_recv, f_mid, f_out,
    send_sem, recv_sem, load_sem,
):
    dp, mp = lax.axis_index("dp"), lax.axis_index("mp")
    y = lax.rem(dp, 8)
    zx = lax.div(dp, 8)
    zl, x = lax.div(zx, 4), lax.rem(zx, 4)
    zh, core = lax.div(mp, 2), lax.rem(mp, 2)
    sib = zh * 2 + 1 - core
    up, down = lax.rem(zh + 1, 4) * 2 + core, lax.rem(zh + 3, 4) * 2 + core
    far = lax.rem(zh + 2, 4) * 2 + core
    sib_up, sib_down = lax.rem(zh + 1, 4) * 2 + 1 - core, lax.rem(zh + 3, 4) * 2 + 1 - core
    sib_far = lax.rem(zh + 2, 4) * 2 + 1 - core

    index_of = {"mp": mp, "y": y, "zx": zx}
    device_of = {
        "mp": lambda p: (dp, p),
        "y": lambda p: (zx * 8 + p, mp),
        "zx": lambda p: (p * 8 + y, mp),
    }
    used = [0]
    started = []

    def tag():
        used[0] += 1
        return used[0] - 1

    def remote(src, dst, number, device):
        return pltpu.make_async_remote_copy(
            src_ref=src, dst_ref=dst, send_sem=send_sem.at[number], recv_sem=recv_sem.at[number],
            device_id=device, device_id_type=MESH,
        )

    def send(src, dst, number, device):
        copy = remote(src, dst, number, device)
        copy.start()
        started.append(copy)

    def landed(region, number):
        remote(region, region, number, (dp, sib)).wait_recv()

    def spread(kind, src, dst, seven):
        me, number = index_of[kind], tag()
        for k in range(1, 8):
            peer = lax.rem(me + k, 8)
            remote(src(peer), dst, number, device_of[kind](peer)).start()
        started.append(remote(seven, seven, number, (dp, sib)))
        return number, seven

    def collect(ticket):
        landed(ticket[1], ticket[0])

    loads = [
        pltpu.make_async_copy(src, dst, load_sem.at[i])
        for i, (src, dst) in enumerate(((w_in, w), (h_in, h), (a_in, a), (b_in, b)))
    ]

    barrier = pltpu.get_barrier_semaphore()
    for kind in ("mp", "y", "zx"):
        for k in range(1, 8):
            pl.semaphore_signal(barrier, inc=1, device_id=device_of[kind](lax.rem(index_of[kind] + k, 8)), device_id_type=MESH)
    for copy in loads:
        copy.start()
    pb[zx, y] = jnp.full((1, 128), pos[0].astype(F32), F32)
    first7 = pl.ds(0, 7)
    loads[0].wait()
    wf[zl, x, y] = w[...]
    for copy in loads[1:]:
        copy.wait()
    low_t = mm(a[...], h[...], NT)
    for o in range(8):
        low_part[o] = low_t[16 * (o // 4) : 16 * (o // 4) + 16, 128 * (o % 4) : 128 * (o % 4) + 128].astype(BF16)
    low_recv[mp] = low_part[mp]
    pl.semaphore_wait(barrier, 21)

    w_z = tag()
    send(w, wf.at[zl, x, y], w_z, ((1 - zl) * 32 + x * 8 + y, mp))

    low_tags = spread("mp", lambda p: low_part.at[p], low_recv.at[mp], low_recv.at[first7])

    def half(q):
        return pl.ds(256 * q, 256)

    pos_y = spread("y", lambda p: pb.at[zx, y], pb.at[zx, y], pb.at[zx, first7])

    def device_x(k):
        return (zl * 32 + lax.rem(x + k, 4) * 8 + y, mp)

    def device_y(k):
        return (zx * 8 + lax.rem(y + k, 8), mp)

    def ring_x(view):
        tags = [tag() for _ in range(6)]
        before, after, across = lax.rem(x + 3, 4), lax.rem(x + 1, 4), lax.rem(x + 2, 4)

        def first(z):
            send(view(x, z), view(x, z), tags[(0, 2)[z]], device_x(1))
            send(view(x, z), view(x, z), tags[(3, 1)[z]], device_x(3))

        def second():
            landed(view(before, 0), tags[0])
            send(view(before, 0), view(before, 0), tags[4], device_x(1))
            landed(view(after, 1), tags[1])
            send(view(after, 1), view(after, 1), tags[5], device_x(3))

        def last():
            landed(view(before, 1), tags[2])
            landed(view(after, 0), tags[3])
            landed(view(across, 0), tags[4])
            landed(view(across, 1), tags[5])

        return first, second, last

    def ring_y(chunk, chunks):
        ups = [[tag() for _ in range(4)] for _ in chunks]
        downs = [[tag() for _ in range(4)] for _ in chunks]

        def step(j, z):
            below, above = chunk(lax.rem(y + 8 - j, 8), z), chunk(lax.rem(y + j, 8), z)
            last_up, last_down = chunks[z]
            if 0 < j < 4 or (j == 4 and last_up):
                landed(below, ups[z][j - 1])
            if 0 < j < 4 or (j == 4 and last_down):
                landed(above, downs[z][j - 1])
            if j < 3 or (j == 3 and last_up):
                send(below, below, ups[z][j], device_y(1))
            if j < 3 or (j == 3 and last_down):
                send(above, above, downs[z][j], device_y(7))

        return step

    rows_a, rows_b = pl.ds(0, 32), pl.ds(32, 32)
    plane = (zl, 1 - zl)
    a_x = ring_x(lambda xx, z: wf.at[plane[z], xx, y, rows_a])
    a_y = ring_y(lambda yy, z: wf.at[plane[z], :, yy, rows_a], ((True, False), (False, True)))
    b_y = ring_y(lambda yy, z: wf.at[plane[z], x, yy, rows_b], ((True, False), (False, True)))
    b_x = ring_x(lambda xx, z: wf.at[plane[z], xx, :, rows_b])

    f_up, f_down = tag(), tag()
    s_tags = {key: tag() for key in ("d0", "d1", "u0", "u1", "f0", "f1")}

    def pass_on():
        landed(hid.at[down, half(0)], h_up[0])
        send(hid.at[down, half(0)], hid.at[down, half(0)], f_up, (dp, up))
        landed(hid.at[up, half(1)], h_down[1])
        send(hid.at[up, half(1)], hid.at[up, half(1)], f_down, (dp, down))

    def to_sib(owner, q, key):
        send(hid.at[owner, half(q)], hid.at[owner, half(q)], s_tags[key], (dp, sib))

    a_x[0](0)
    b_y(0, 0)
    landed(wf.at[1 - zl, x, y], w_z)
    a_x[0](1)
    b_y(0, 1)

    h_up, h_down = [tag() for _ in range(2)], [tag() for _ in range(2)]
    h_sib = tag()
    for q in range(2):
        send(h.at[half(q)], hid.at[mp, half(q)], h_up[q], (dp, up))
        send(h.at[half(1 - q)], hid.at[mp, half(1 - q)], h_down[1 - q], (dp, down))
    send(h, hid.at[mp], h_sib, (dp, sib))

    b_y(1, 0)
    b_y(1, 1)
    a_x[1]()
    a_x[2]()
    a_y(0, 0)
    a_y(0, 1)
    collect(low_tags)
    low_full[mp] = jnp.sum(low_recv[...].astype(F32), axis=0).astype(BF16)
    low_all = spread("mp", lambda p: low_full.at[mp], low_full.at[mp], low_full.at[first7])
    b_y(2, 0)
    b_y(2, 1)
    collect(pos_y)
    pos_zx = spread("zx", lambda p: pb.at[zx], pb.at[zx], pb.at[first7])
    b_y(3, 0)
    b_y(3, 1)
    a_y(1, 0)
    b_y(4, 0)
    b_x[0](0)
    b_y(4, 1)
    b_x[0](1)
    a_y(1, 1)
    a_y(2, 0)
    row_of = lax.broadcasted_iota(jnp.int32, (256, 1024), 0)
    col_of = lax.broadcasted_iota(jnp.int32, (256, 1024), 1)
    slot_of = ((lax.shift_right_logical(col_of, 4) * 4 + (col_of & 3)) == row_of).astype(F32).astype(BF16)
    numbers8 = jnp.broadcast_to(assign_row[...].astype(F32), (8, 256)).astype(BF16)
    number_of = mm(numbers8, slot_of)[0:1].astype(jnp.int32)
    one_hot[...] = (row_of == number_of).astype(F32).astype(BF16)

    pass_on()
    b_x[1]()
    a_y(2, 1)
    to_sib(down, 0, "d0")
    to_sib(up, 1, "u1")
    landed(hid.at[down, half(1)], h_up[1])
    landed(hid.at[up, half(0)], h_down[0])
    to_sib(down, 1, "d1")
    to_sib(up, 0, "u0")
    a_y(3, 0)
    a_y(3, 1)

    def joined(ref):
        halves = [jnp.concatenate([ref[4 * r + t] for t in range(4)], axis=1) for r in range(2)]
        return jnp.concatenate(halves, axis=0)

    collect(low_all)
    collect(pos_zx)
    low = joined(low_full)
    low_rows = low.astype(F32).T.astype(BF16)
    acc[...] = adapter_factor_scale * mm(low_rows, b[...])
    landed(hid.at[sib], h_sib)
    b_x[2]()
    a_y(4, 0)
    a_y(4, 1)

    def slab(m):
        return wf[lax.div(m, 4), lax.rem(m, 4)].reshape(512, 512)

    def tokens(i):
        return pl.ds(pl.multiple_of(256 * i, 256), 256)

    @pl.loop(0, 2)
    def _(i):
        t = tokens(i)
        acc[t] += mm(h[t], slab(mp)) + mm(hid[sib, t], slab(sib))

    landed(hid.at[far, half(0)], f_up)
    to_sib(far, 0, "f0")
    landed(hid.at[far, half(1)], f_down)
    to_sib(far, 1, "f1")
    landed(hid.at[sib_down, half(0)], s_tags["d0"])
    landed(hid.at[sib_up, half(1)], s_tags["u1"])
    landed(hid.at[sib_down, half(1)], s_tags["d1"])
    landed(hid.at[sib_up, half(0)], s_tags["u0"])

    @pl.loop(0, 2)
    def _(i):
        t = tokens(i)
        total = acc[t]
        for m in (down, up, sib_down, sib_up):
            total += mm(hid[m, t], slab(m))
        acc[t] = total

    landed(hid.at[sib_far, half(0)], s_tags["f0"])
    landed(hid.at[sib_far, half(1)], s_tags["f1"])

    ones = jnp.ones((8, 128), BF16)

    @pl.loop(0, 2)
    def _(i):
        t = tokens(i)
        total = acc[t] + h[t].astype(F32)
        for m in (far, sib_far):
            total += mm(hid[m, t], slab(m))
        pre[t] = total.astype(BF16)
        squares = total * total
        squares = squares[:, 0:128] + squares[:, 128:256] + squares[:, 256:384] + squares[:, 384:512]
        high = squares.astype(BF16)
        rest = (squares - high.astype(F32)).astype(BF16)
        sq_row[i] = mm(ones, high, NT) + mm(ones, rest, NT)

    row8 = lax.broadcasted_iota(jnp.int32, (8, 128), 0)
    lane8 = lax.broadcasted_iota(jnp.int32, (8, 128), 1)

    def by_sequence(wide):
        value = jnp.zeros((8, 128), F32)
        for s in range(4):
            value = jnp.where(lax.rem(row8, 4) == s, wide[:, 128 * s : 128 * s + 128], value)
        return value

    def diagonal(value, first, every):
        keep = lax.rem(row8, 4) if every else row8 - first
        return jnp.concatenate([jnp.where(keep == s, value, 0.0) for s in range(4)], axis=1)

    sq[mp] = by_sequence(jnp.concatenate([sq_row[0], sq_row[1]], axis=1))
    sq_tags = spread("mp", lambda p: sq.at[mp], sq.at[mp], sq.at[first7])

    p_t = mm(b[...], pre[...], NT)
    for o in range(8):
        p_part[o] = p_t[16 * (o // 4) : 16 * (o // 4) + 16, 128 * (o % 4) : 128 * (o % 4) + 128].astype(BF16)
    p_tags = spread("mp", lambda p: p_part.at[p], p_recv.at[mp], p_recv.at[first7])
    p_recv[mp] = p_part[mp]

    lengths = jnp.zeros((8, 128), jnp.int32)
    mine = jnp.zeros((8, 256), jnp.int32)
    row256 = lax.broadcasted_iota(jnp.int32, (8, 256), 0)
    lane256 = lax.broadcasted_iota(jnp.int32, (8, 256), 1)
    for s in range(4):
        number = assign[dp * 4 + s]
        lengths = jnp.where(lax.rem(row8, 4) == s, counts[number], lengths)
        mine = jnp.where(lax.rem(row256, 4) == s, number, mine)
    weight = jnp.where(lane8 < lengths, 1.0, 0.0) / lengths.astype(F32)

    collect(sq_tags)
    inv_rms = lax.rsqrt(jnp.sum(sq[...], axis=0) / WIDTH + 1e-05)
    alpha = weight * inv_rms
    mean = mm_split(diagonal(alpha, 0, True), pre[...])
    tile = [
        jnp.where(row8 < 4, mean[:, 256 * j : 256 * j + 128], mean[:, 256 * j + 128 : 256 * j + 256])
        for j in range(2)
    ]
    pooled[zx, y] = jnp.concatenate(tile, axis=0).astype(BF16)

    y_tags = spread("y", lambda p: pooled.at[zx, y], pooled.at[zx, y], pooled.at[zx, first7])
    collect(p_tags)
    p_full[mp] = jnp.sum(p_recv[...].astype(F32), axis=0).astype(BF16)
    p_all = spread("mp", lambda p: p_full.at[mp], p_full.at[mp], p_full.at[first7])
    collect(y_tags)
    zx_tags = spread("zx", lambda p: pooled.at[zx], pooled.at[zx], pooled.at[first7])
    collect(zx_tags)
    row16 = lax.shift_right_logical(lax.broadcasted_iota(jnp.int32, (16, 128), 0), 2)
    gathered = pooled[...].reshape(64, 16, 128)
    chosen = [(gathered * (row16 == j).astype(F32).astype(BF16)[None]).reshape(1024, 128) for j in range(4)]
    units[...] = mm(one_hot[...], jnp.concatenate(chosen, axis=1)).astype(BF16)

    x_part[...] = mm(units[0:64], units[...], NT).reshape(8, 8, 256)
    x_tags = spread("mp", lambda p: x_part.at[p], x_recv.at[mp], x_recv.at[first7])
    square = units[...].astype(F32)
    square = square * square
    high = square.astype(BF16)
    rest = (square - high.astype(F32)).astype(BF16)
    ones_wide = jnp.ones((8, 512), BF16)
    n_recv[mp] = (mm(ones_wide, high, NT) + mm(ones_wide, rest, NT))[0:1]
    n_tags = spread("mp", lambda p: n_recv.at[mp], n_recv.at[mp], n_recv.at[first7])
    x_recv[mp] = x_part[mp]
    collect(x_tags)
    x_full[mp] = jnp.sum(x_recv[...], axis=0)
    g_tags = spread("mp", lambda p: x_full.at[mp], x_full.at[mp], x_full.at[first7])
    collect(n_tags)
    lengths_sq = n_recv[0]
    for s in range(1, 8):
        lengths_sq = lengths_sq + n_recv[s]
    inv_norm = 1.0 / jnp.sqrt(lengths_sq + 1e-06)
    rowq = lax.broadcasted_iota(jnp.int32, (64, 256), 0)
    laneq = lax.broadcasted_iota(jnp.int32, (64, 256), 1)
    inv_query = jnp.sum(jnp.where(rowq == laneq, inv_norm, 0.0), axis=1, keepdims=True)
    scale = score_scale * inv_query * inv_norm
    document = laneq >= 64
    positive = pb[...].reshape(64, 1, 128)[:, 0, :]
    positive = jnp.concatenate([positive, positive], axis=1)
    positive_mask = jnp.where((laneq - 64).astype(F32) == positive, 1.0, 0.0)
    collect(g_tags)

    scores = jnp.where(document, scale * x_full[...].reshape(64, 256), 0.0)
    exponents = jnp.where(document, jnp.exp(scores), 0.0)
    exp_total = jnp.sum(exponents, axis=1, keepdims=True)
    query_loss = jnp.log(exp_total) - jnp.sum(positive_mask * scores, axis=1, keepdims=True)
    loss[0] = jnp.sum(jnp.where(rowq[:, 0:1] == dp, query_loss, 0.0))
    score_grads = exponents / exp_total - positive_mask
    inner = score_grads * scores
    inner_query = jnp.sum(inner, axis=1, keepdims=True)
    inner_document = jnp.sum(inner, axis=0, keepdims=True)
    coef = scale * score_grads

    below = jnp.zeros((192, 256), F32)
    coef_query = coef - jnp.where(rowq == laneq, inner_query * inv_query * inv_query, 0.0)
    own = (lane256 == mine).astype(F32)
    own_document = jnp.where(lane256 >= 64, own, 0.0)

    def picked(rows, matrix, dims):
        matrix = jnp.concatenate([matrix, below], axis=0)
        top = matrix.astype(BF16)
        return mm(rows, top, dims) + mm(rows, (matrix - top.astype(F32)).astype(BF16), dims)

    mix = (
        picked(own.astype(BF16), coef_query, NN)
        + picked(own_document.astype(BF16), coef, NT)
        - own_document * (inner_document * inv_norm * inv_norm)
    )
    grad = mm_split(mix, units[...])

    b_wide = jnp.concatenate([b[...].astype(F32), jnp.zeros((96, 512), F32)], axis=0).astype(BF16)
    ex[mp] = jnp.where(row8 < 4, by_sequence(mm_split(grad, pre[...], NT)), mm_split(grad, b_wide, NT))
    e_tags = spread("mp", lambda p: ex.at[mp], ex.at[mp], ex.at[first7])
    alpha_top, alpha_low = diagonal(alpha, 0, False), diagonal(alpha, 4, False)
    low_grad = mm_exact(mm_exact(low.astype(F32), alpha_top, NT), grad)
    collect(p_all)
    p_rows = joined(p_full).astype(F32)
    collect(e_tags)
    total = jnp.sum(ex[...], axis=0)
    beta = inv_rms * inv_rms * alpha * total / WIDTH
    beta_row = jnp.sum(diagonal(beta, 0, False), axis=0, keepdims=True)
    up_grad = mm_exact(total.T[0:32], alpha_low)
    grad_low = (adapter_factor_scale * (up_grad - p_rows * beta_row)).astype(BF16)
    part_a = mm(grad_low, h[...])
    part_b = adapter_factor_scale * (low_grad - mm((low.astype(F32) * beta_row).astype(BF16), pre[...]))

    total = jnp.concatenate([part_a, part_b], axis=0).astype(BF16)
    for o in range(8):
        f_part[o] = total[16 * (o // 2) : 16 * (o // 2) + 16, 256 * (o % 2) : 256 * (o % 2) + 256]
    tags1 = spread("zx", lambda p: f_part.at[p], f_recv.at[zx], f_recv.at[first7])
    f_recv[zx] = f_part[zx]
    collect(tags1)
    f_mid[y] = jnp.sum(f_recv[...].astype(F32), axis=0).astype(BF16)
    tags2 = spread("y", lambda p: f_mid.at[y], f_mid.at[y], f_mid.at[first7])
    collect(tags2)
    f_out[zx] = jnp.sum(f_mid[...].astype(F32), axis=0).astype(BF16)
    tags3 = spread("zx", lambda p: f_out.at[zx], f_out.at[zx], f_out.at[first7])
    collect(tags3)
    for o in range(8):
        place = pl.ds(16 * (o // 2 % 2), 16), pl.ds(256 * (o % 2), 256)
        (grad_a if o < 4 else grad_b)[place] = f_out[o].astype(F32)

    for copy in started:
        copy.wait_send()
    assert used[0] == TAGS, used[0]


def body(hidden, frozen_matrix, adapter_down_weight, adapter_up_weight, sequence_token_counts, assignment, positives):
    vmem, smem = pl.BlockSpec(memory_space=pltpu.VMEM), pl.BlockSpec(memory_space=pltpu.SMEM)
    anywhere = pl.BlockSpec(memory_space=pltpu.HBM)
    V = pltpu.VMEM
    loss, grad_a, grad_b = pl.pallas_call(
        kernel,
        out_shape=(
            jax.ShapeDtypeStruct((1,), F32),
            jax.ShapeDtypeStruct((32, 512), F32),
            jax.ShapeDtypeStruct((32, 512), F32),
        ),
        in_specs=[anywhere, anywhere, anywhere, anywhere, smem, smem, smem, vmem],
        out_specs=(smem, vmem, vmem),
        scratch_shapes=[
            V((512, 512), BF16),
            V((64, 512), BF16),
            V((32, 512), BF16),
            V((32, 512), BF16),
            V((8, 512, 512), BF16),
            V((2, 4, 8, 64, 512), BF16),
            V((8, 16, 128), BF16),
            V((8, 16, 128), BF16),
            V((8, 16, 128), BF16),
            V((8, 8, 1, 128), F32),
            V((512, 512), F32),
            V((512, 512), BF16),
            V((2, 8, 256), F32),
            V((256, 1024), BF16),
            V((8, 8, 128), F32),
            V((8, 16, 128), BF16),
            V((8, 16, 128), BF16),
            V((8, 16, 128), BF16),
            V((8, 8, 16, 128), BF16),
            V((256, 512), BF16),
            V((8, 8, 256), F32),
            V((8, 8, 256), F32),
            V((8, 8, 256), F32),
            V((8, 1, 256), F32),
            V((8, 8, 128), F32),
            V((8, 16, 256), BF16),
            V((8, 16, 256), BF16),
            V((8, 16, 256), BF16),
            V((8, 16, 256), BF16),
            pltpu.SemaphoreType.DMA((TAGS,)),
            pltpu.SemaphoreType.DMA((TAGS,)),
            pltpu.SemaphoreType.DMA((4,)),
        ],
        compiler_params=pltpu.CompilerParams(
            collective_id=0, has_side_effects=True, vmem_limit_bytes=60 * 1024 * 1024
        ),
    )(
        hidden.reshape(512, 512),
        frozen_matrix,
        adapter_down_weight.T,
        adapter_up_weight,
        positives,
        sequence_token_counts,
        assignment,
        assignment.reshape(1, 256),
    )
    return loss, grad_a.T, grad_b


def solution(mesh):
    return jax.shard_map(
        body,
        mesh=mesh,
        in_specs=(
            P("dp", None, "mp"),
            P("dp", "mp"),
            P("mp", None),
            P(None, "mp"),
            P(),
            P(),
            P("dp"),
        ),
        out_specs=(P("dp"), P("mp", None), P(None, "mp")),
        check_vma=False,
    )
```
